1024 devices in a mesh: blocks: 128 (over y, z, core), sub: 8 (over x).
Axes of the slice: x: 8, y: 8, z: 8, core: 2. Of those that a mesh axis runs over, the one named last changes fastest.
Arguments:
- state: float32 [128, 8, 3, 5, 4096], P('blocks', 'sub'), may hold values from -2.5 to 10, as said below
- neighbours: int32 [128, 8, 3, 6, 2], P('blocks', 'sub'), may hold values from 0 to 3, as said below
- counts: int32 [128, 8], P('blocks'), may hold values from 1 to 3, as said below
Outputs:
- new_state: float32 [128, 8, 3, 5, 4096], P('blocks', 'sub')
The draws below stay inside these ranges and needn't reach their ends.
Inputs may be any that keep to these rules, and one draw needn't show every extreme that they name: `counts`: A device's live blocks are its slots 0 to count - 1; some device holds 3 blocks and some hold one. `neighbours`: component 0 is 0, 1 or 2 for a neighbour block on the device at blocks index - 1, the same, or + 1 (same sub index), and 3 for a face on the domain's boundary; component 1 is then a live slot of that device, and 0 on the boundary. Entries of slots that are not live follow the same rule. No entry points past either end of the blocks axis. Every slot holds a physical state: density and pressure (heat ratio 1.4) lie in [0.4, 2.5], each velocity component in [-1, 1].
All inputs are finite; a program needn't handle non-finite values.
Results may differ from the reference program's by a relative error of at most 0.0003.
Values sent between devices are 32-bit elements; how exact they have to be, the bound alone decides.
No kernel may reach another device: no remote copies, remote signals or barrier semaphores. Data moves between devices by JAX's collectives and lax.ppermute only.
A program may use at most 32 MiB of HBM per device.

```python
import jax
import jax.numpy as jnp
from jax import lax

EDGE = 16
FIELDS = 5
SLOTS = 3
ROUNDS = 3
N_BLOCKS = 128
N_SUB = 8


def block_counts(key):
    pick_full = jax.random.randint(jax.random.fold_in(key, 101), (N_BLOCKS, N_SUB), 0, 20)
    low_count = 1 + jax.random.randint(jax.random.fold_in(key, 102), (N_BLOCKS, N_SUB), 0, 2)
    counts = jnp.where(pick_full < 3, SLOTS, jnp.minimum(low_count, SLOTS))
    counts = counts.at[0, 0].set(SLOTS).at[0, 1].set(1)
    return counts.astype(jnp.int32)


def draw_counts(key, part):
    counts = block_counts(key)
    return counts


def draw_neighbours(key, part):
    counts = block_counts(key)
    key = jax.random.fold_in(key, 2)
    key_kind, key_slot = jax.random.split(key)
    shape = (N_BLOCKS, N_SUB, SLOTS, 6)
    kind_pick = jax.random.randint(key_kind, shape, 0, 8)
    owner_code = jnp.where(kind_pick < 2, 0, jnp.where(kind_pick < 4, 2, jnp.where(kind_pick < 7, 1, 3)))
    row_number = jnp.arange(N_BLOCKS, dtype=jnp.int32)[:, None, None, None]
    owner_code = jnp.where((row_number == 0) & (owner_code == 0), 1, owner_code)
    owner_code = jnp.where((row_number == N_BLOCKS - 1) & (owner_code == 2), 1, owner_code)
    source_row = jnp.clip(row_number + owner_code - 1, 0, N_BLOCKS - 1)
    column = jnp.arange(N_SUB, dtype=jnp.int32)[None, :, None, None]
    source_count = counts[source_row, column]
    raw_draw = jax.random.randint(key_slot, shape, 0, 1 << 20)
    slot_pick = jnp.where(owner_code == 3, 0, raw_draw % source_count)
    owner_code = owner_code.at[1, 0, 0, 0].set(0)
    slot_pick = slot_pick.at[1, 0, 0, 0].set(SLOTS - 1)
    return jnp.stack([owner_code, slot_pick], axis=-1).astype(jnp.int32)


def draw_state(key, part):
    key = jax.random.fold_in(key, 3)
    subkeys = jax.random.split(key, 3)
    shape = (N_BLOCKS, N_SUB, SLOTS, EDGE ** 3)
    lowest, highest, speed = (0.5, 2.0, 0.6)
    density = jnp.exp(jax.random.uniform(subkeys[0], shape, jnp.float32, jnp.log(lowest), jnp.log(highest)))
    pressure = jnp.exp(jax.random.uniform(subkeys[1], shape, jnp.float32, jnp.log(lowest), jnp.log(highest)))
    velocity = jax.random.uniform(subkeys[2], (3,) + shape, jnp.float32, -speed, speed)
    energy = pressure / 0.4 + 0.5 * density * jnp.sum(velocity * velocity, axis=0)
    fields = jnp.stack([density, density * velocity[0], density * velocity[1], density * velocity[2], energy], axis=3)
    return fields.astype(jnp.float32)


def setup_inputs(seed: int = 0) -> dict:
    streams_of = jax.random.split(jax.random.key(seed), 4)
    return {
        "state": draw_state(jax.random.fold_in(streams_of[3], 71), 0),
        "neighbours": draw_neighbours(jax.random.fold_in(streams_of[3], 71), 0),
        "counts": draw_counts(jax.random.fold_in(streams_of[3], 71), 0),
    }


heat_ratio = 1.4
courant = 0.07

def block_faces(block):
    block_cube = block.reshape(FIELDS, EDGE, EDGE, EDGE)
    low_x = block_cube[:, 0:2]
    high_x = block_cube[:, EDGE - 2:][:, ::-1]
    low_y = jnp.transpose(block_cube[:, :, 0:2], (0, 2, 1, 3))
    high_y = jnp.transpose(block_cube[:, :, EDGE - 2:][:, :, ::-1], (0, 2, 1, 3))
    low_z = jnp.transpose(block_cube[:, :, :, 0:2], (0, 3, 1, 2))
    high_z = jnp.transpose(block_cube[:, :, :, EDGE - 2:][:, :, :, ::-1], (0, 3, 1, 2))
    face_layers = jnp.stack([low_x, high_x, low_y, high_y, low_z, high_z], axis=0)
    return face_layers.reshape(6, FIELDS, 2 * EDGE * EDGE)

def pick_ghosts(window, face_links, slot_total):
    owner_code = face_links[..., 0]
    source = face_links[..., 1]
    own_slot = jnp.arange(slot_total, dtype=jnp.int32)[:, None]
    face_number = jnp.arange(6, dtype=jnp.int32)[None, :]
    boundary = owner_code == 3
    device = jnp.where(boundary, 1, owner_code)
    slot_index = jnp.where(boundary, own_slot, source)
    face_side = jnp.where(boundary, face_number, face_number ^ 1)
    flat_index = ((device * slot_total + slot_index) * 6 + face_side).astype(jnp.int32)
    flattened = window.reshape(3 * slot_total * 6, FIELDS, -1)
    picked = jnp.take(flattened, flat_index.reshape(-1), axis=0)
    return picked.reshape(slot_total, 6, FIELDS, -1)

def primitives(conserved_cells):
    density = conserved_cells[0]
    velocity = conserved_cells[1:4] / density
    pressure = (heat_ratio - 1.0) * (conserved_cells[4] - 0.5 * density * lax.optimization_barrier(jnp.sum(velocity * velocity, axis=0)))
    return jnp.concatenate([density[None], velocity, pressure[None]], axis=0)

def to_conserved(prim):
    density = prim[0]
    velocity = prim[1:4]
    energy = prim[4] / (heat_ratio - 1.0) + 0.5 * density * lax.optimization_barrier(jnp.sum(velocity * velocity, axis=0))
    return jnp.concatenate([density[None], density[None] * velocity, energy[None]], axis=0)

def physical(prim, conserved_cells, along):
    normal = prim[along]
    pressure = prim[4]
    components = [conserved_cells[number] * normal for number in range(5)]
    components[along] = components[along] + pressure
    components[4] = components[4] + pressure * normal
    return jnp.stack(components, axis=0)

def hll_flux(left_state, right_state, along):
    sound_left = jnp.sqrt(heat_ratio * left_state[4] / left_state[0])
    sound_right = jnp.sqrt(heat_ratio * right_state[4] / right_state[0])
    speed_left = left_state[along]
    speed_right = right_state[along]
    slow_speed = jnp.minimum(jnp.minimum(speed_left - sound_left, speed_right - sound_right), 0.0)
    fast_speed = jnp.maximum(jnp.maximum(speed_left + sound_left, speed_right + sound_right), 0.0)
    cons_left = to_conserved(left_state)
    cons_right = to_conserved(right_state)
    flux_left = physical(left_state, cons_left, along)
    flux_right = physical(right_state, cons_right, along)
    return (fast_speed * flux_left - slow_speed * flux_right + slow_speed * fast_speed * (cons_right - cons_left)) / (fast_speed - slow_speed)

def cut_along(values, first_cell, last_cell, along):
    return lax.slice_in_dim(values, first_cell, last_cell, axis=along)

def minmod(first_diff, second_diff):
    smaller = jnp.where(jnp.abs(first_diff) < jnp.abs(second_diff), first_diff, second_diff)
    return jnp.where(first_diff * second_diff > 0, smaller, 0.0)

def axis_change(prim, along):
    length = prim.shape[along]
    differences = cut_along(prim, 1, length, along) - cut_along(prim, 0, length - 1, along)
    slopes = minmod(cut_along(differences, 0, length - 2, along), cut_along(differences, 1, length - 1, along))
    centres = cut_along(prim, 1, length - 1, along)
    left_state = cut_along(centres + 0.5 * slopes, 0, EDGE + 1, along)
    right_state = cut_along(centres - 0.5 * slopes, 1, EDGE + 2, along)
    fluxes = hll_flux(left_state, right_state, along)
    return cut_along(fluxes, 1, EDGE + 1, along) - cut_along(fluxes, 0, EDGE, along)

def update_block(block, ghosts):
    block_cube = block.reshape(FIELDS, EDGE, EDGE, EDGE)
    shaped = ghosts.reshape(6, FIELDS, 2, EDGE, EDGE)
    lower_side, upper_side = (shaped[0], shaped[1])
    padded = jnp.concatenate([lower_side[:, 1:2], lower_side[:, 0:1], block_cube, upper_side[:, 0:1], upper_side[:, 1:2]], axis=1)
    change = axis_change(primitives(padded), 1)
    lower_side, upper_side = (shaped[2], shaped[3])
    padded = jnp.concatenate([lower_side[:, 1][:, :, None], lower_side[:, 0][:, :, None], block_cube, upper_side[:, 0][:, :, None], upper_side[:, 1][:, :, None]], axis=2)
    change = change + axis_change(primitives(padded), 2)
    lower_side, upper_side = (shaped[4], shaped[5])
    padded = jnp.concatenate([lower_side[:, 1][..., None], lower_side[:, 0][..., None], block_cube, upper_side[:, 0][..., None], upper_side[:, 1][..., None]], axis=3)
    change = change + axis_change(primitives(padded), 3)
    return (block_cube - courant * change).reshape(FIELDS, -1)

def rebalance(row_blocks, row_counts):
    positions = jnp.arange(N_SUB, dtype=jnp.int32)
    slot_range = jnp.arange(SLOTS, dtype=jnp.int32)[None, :]
    for bit_number in range(ROUNDS):
        partner = positions ^ 1 << bit_number
        own_count = row_counts
        theirs = row_counts[partner]
        handed = jnp.where(own_count > theirs, (own_count - theirs) // 2, 0)
        taken = jnp.where(theirs > own_count, (theirs - own_count) // 2, 0)
        partner_blocks = row_blocks[partner]
        first_sent = (theirs - taken)[:, None]
        source = jnp.clip(first_sent + slot_range - own_count[:, None], 0, SLOTS - 1).astype(jnp.int32)
        moved_items = jnp.take_along_axis(partner_blocks, source[:, :, None, None], axis=1)
        incoming = (slot_range >= own_count[:, None]) & (slot_range < (own_count + taken)[:, None])
        row_blocks = jnp.where(incoming[:, :, None, None], moved_items, row_blocks)
        row_counts = own_count - handed + taken
    live_mask = slot_range < row_counts[:, None]
    return jnp.where(live_mask[:, :, None, None], row_blocks, jnp.zeros_like(row_blocks))

def reference(state, neighbours, counts):
    face_layers = jax.vmap(jax.vmap(jax.vmap(block_faces)))(state)
    zero_rim = jnp.zeros_like(face_layers[:1])
    padded_faces = jnp.concatenate([zero_rim, face_layers, zero_rim], axis=0)

    def one_row(row_index):
        window = lax.dynamic_slice_in_dim(padded_faces, row_index, 3, 0)
        row_blocks = state[row_index]
        row_links = neighbours[row_index]
        ghosts = jax.vmap(lambda part_window, part_links: pick_ghosts(part_window, part_links, SLOTS), in_axes=(1, 0))(window, row_links)
        updated = jax.vmap(jax.vmap(update_block))(row_blocks, ghosts)
        return rebalance(updated, counts[row_index])
    return lax.map(one_row, jnp.arange(N_BLOCKS, dtype=jnp.int32))
```

```python
import functools

import jax
import jax.numpy as jnp
from jax import lax
from jax.experimental import pallas as pl
from jax.experimental.pallas import tpu as pltpu
from jax.sharding import PartitionSpec as P

EDGE = 16
FIELDS = 5
SLOTS = 3
LANES = 128
ROWS = 2 * SLOTS
CHUNKS = 32
FACE_ROWS = 6 * 2 * FIELDS * ROWS

heat_ratio = 1.4
courant = 0.07

VMEM_LIMIT = 48 * 1024 * 1024


def swap_chunks(planes, width, lane):
    planes = list(planes)
    step = 1
    while step < len(planes):
        upper = (lane & (step * width)) != 0
        for low in range(len(planes)):
            if low & step:
                continue
            a, b = planes[low], planes[low + step]
            planes[low] = jnp.where(upper, pltpu.roll(b, step * width, 1), a)
            planes[low + step] = jnp.where(upper, b, pltpu.roll(a, LANES - step * width, 1))
        step *= 2
    return planes


def swap_halves(planes, row):
    odd = (row & 1) != 0
    half = len(planes) // 2
    first = [jnp.where(odd, pltpu.roll(b, 1, 0), a) for a, b in zip(planes[:half], planes[half:])]
    second = [jnp.where(odd, b, pltpu.roll(a, 7, 0)) for a, b in zip(planes[:half], planes[half:])]
    return first + second


def tile_iotas():
    return (
        lax.broadcasted_iota(jnp.int32, (8, LANES), 1),
        lax.broadcasted_iota(jnp.int32, (8, LANES), 0),
    )


def x_to_y(planes, lane, row):
    planes = swap_chunks(planes[:8], EDGE, lane) + swap_chunks(planes[8:], EDGE, lane)
    return swap_halves(planes, row)


def y_to_x(planes, lane, row):
    planes = swap_halves(planes, row)
    return swap_chunks(planes[:8], EDGE, lane) + swap_chunks(planes[8:], EDGE, lane)


def prepare_kernel(state, planes, faces, work):
    for slot in range(SLOTS):
        for chunk in range(CHUNKS):
            base = (chunk // 2) * FIELDS * 8 + 2 * slot + chunk % 2
            work[pl.ds(base, FIELDS, stride=8), :] = state[
                0, 0, slot, :, chunk * LANES : (chunk + 1) * LANES
            ]
    for number in range(EDGE):
        base = number * FIELDS * 8
        rows = [work[base + 8 * field : base + 8 * field + 8, :] for field in range(FIELDS)]
        inverse = 1.0 / rows[0]
        v1, v2, v3 = rows[1] * inverse, rows[2] * inverse, rows[3] * inverse
        pressure = (heat_ratio - 1.0) * (
            rows[4] - 0.5 * rows[0] * (v1 * v1 + v2 * v2 + v3 * v3)
        )
        for field, value in enumerate((rows[0], v1, v2, v3, pressure)):
            planes[0, number, field] = value

    lane, row = tile_iotas()

    def one_field(field, carry):
        x_planes = [planes[0, number, field] for number in range(EDGE)]
        y_planes = x_to_y(x_planes, lane, row)
        for number in range(EDGE):
            planes[1, number, field] = y_planes[number]
        z_planes = swap_chunks(y_planes, 1, lane)
        for number in range(EDGE):
            planes[2, number, field] = z_planes[number]
        return carry

    lax.fori_loop(0, FIELDS, one_field, 0)

    for axis in range(3):
        for side in range(2):
            for depth in range(2):
                number = depth if side == 0 else EDGE - 1 - depth
                for field in range(FIELDS):
                    base = (((2 * axis + side) * 2 + depth) * FIELDS + field) * ROWS
                    faces[base : base + ROWS, :] = planes[axis, number, field, 0:ROWS, :]


def prepare(state):
    return pl.pallas_call(
        prepare_kernel,
        out_shape=(
            jax.ShapeDtypeStruct((3, EDGE, FIELDS, 8, LANES), jnp.float32),
            jax.ShapeDtypeStruct((FACE_ROWS, LANES), jnp.float32),
        ),
        scratch_shapes=[pltpu.VMEM((EDGE * FIELDS * 8, LANES), jnp.float32)],
        compiler_params=pltpu.CompilerParams(vmem_limit_bytes=VMEM_LIMIT),
        name="prepare",
    )(state)


def minmod(first, second):
    return jnp.maximum(jnp.minimum(first, second), 0.0) + jnp.minimum(
        jnp.maximum(first, second), 0.0
    )


def side_speeds(prim, component):
    scaled = heat_ratio * prim[4]
    sound = scaled * lax.rsqrt(scaled * prim[0])
    return prim[component] - sound, prim[component] + sound


def hll_flux(left, right, component):
    slow_left, fast_left = side_speeds(left, component)
    slow_right, fast_right = side_speeds(right, component)
    slow = jnp.minimum(jnp.minimum(slow_left, slow_right), 0.0)
    fast = jnp.maximum(jnp.maximum(fast_left, fast_right), 0.0)
    inverse = 1.0 / (fast - slow)
    weight_left = fast * inverse
    weight_right = -slow * inverse
    product = slow * weight_left
    normal_left, normal_right = left[component], right[component]
    carry_left = weight_left * normal_left - product
    carry_right = weight_right * normal_right + product
    mass_left, mass_right = carry_left * left[0], carry_right * right[0]
    push_left, push_right = weight_left * left[4], weight_right * right[4]
    outputs = [mass_left + mass_right]
    for number in (1, 2, 3):
        value = mass_left * left[number] + mass_right * right[number]
        if number == component:
            value = value + (push_left + push_right)
        outputs.append(value)
    square_left = left[1] * left[1] + left[2] * left[2] + left[3] * left[3]
    square_right = right[1] * right[1] + right[2] * right[2] + right[3] * right[3]
    inner = 1.0 / (heat_ratio - 1.0)
    energy = 0.5 * (mass_left * square_left + mass_right * square_right)
    energy = energy + inner * (carry_left * left[4] + carry_right * right[4])
    energy = energy + (push_left * normal_left + push_right * normal_right)
    outputs.append(energy)
    return outputs


def final_counts(counts, sub_index, rounds):
    size = counts.shape[-1]
    now = [counts[0, position] for position in range(size)]

    def own(values):
        picked = values[0]
        for position in range(1, size):
            picked = jnp.where(sub_index == position, values[position], picked)
        return picked

    start = own(now)
    arrival = jnp.int32(-1)
    for bit in range(rounds):
        gains = [
            jnp.maximum(now[p ^ (1 << bit)] - now[p], 0) // 2
            - jnp.maximum(now[p] - now[p ^ (1 << bit)], 0) // 2
            for p in range(size)
        ]
        arrival = jnp.where(own(gains) > 0, bit, arrival)
        now = [value + gain for value, gain in zip(now, gains)]
    return start, own(now), arrival


def update_kernel(
    rounds, state, planes, own_faces, low_faces, high_faces, links, counts, out, moved, ghosts, change, work
):
    sub_index = lax.axis_index("sub")
    _, last_count, _ = final_counts(counts, sub_index, rounds)

    for face in range(6):
        for slot in range(SLOTS):
            owner = links[0, 0, slot, face, 0]
            boundary = owner == 3
            source = jnp.where(boundary, slot, links[0, 0, slot, face, 1])
            side = jnp.where(boundary, face, face ^ 1)
            for half in range(2):
                base = side * (2 * FIELDS * ROWS) + 2 * source + half
                rows = pl.ds(base, 2 * FIELDS, stride=ROWS)
                values = jnp.where(
                    owner == 0,
                    low_faces[rows, :],
                    jnp.where(owner == 2, high_faces[rows, :], own_faces[rows, :]),
                )
                target = face * (2 * FIELDS * 8) + 2 * slot + half
                ghosts[pl.ds(target, 2 * FIELDS, stride=8), :] = values

    def cell(axis, number):
        if 0 <= number < EDGE:
            return [planes[axis, number, field] for field in range(FIELDS)]
        face = 2 * axis if number < 0 else 2 * axis + 1
        depth = -1 - number if number < 0 else number - EDGE
        base = face * (2 * FIELDS * 8) + depth * FIELDS * 8
        return [ghosts[base + 8 * field : base + 8 * field + 8, :] for field in range(FIELDS)]

    for axis in range(3):
        here = cell(axis, -1)
        diff = [b - a for a, b in zip(cell(axis, -2), here)]
        left, flux = None, None
        for number in range(-1, EDGE + 1):
            after = cell(axis, number + 1)
            next_diff = [b - a for a, b in zip(here, after)]
            half_slope = [0.5 * minmod(a, b) for a, b in zip(diff, next_diff)]
            if left is not None:
                right = [a - b for a, b in zip(here, half_slope)]
                next_flux = hll_flux(left, right, axis + 1)
                if flux is not None:
                    for field in range(FIELDS):
                        change[axis, number - 1, field] = next_flux[field] - flux[field]
                flux = next_flux
            left = [a + b for a, b in zip(here, half_slope)]
            here, diff = after, next_diff

    lane, row = tile_iotas()

    def one_field(field, carry):
        z_change = swap_chunks([change[2, number, field] for number in range(EDGE)], 1, lane)
        y_change = [z_change[number] + change[1, number, field] for number in range(EDGE)]
        x_change = y_to_x(y_change, lane, row)
        for number in range(EDGE):
            base = pl.multiple_of(number * FIELDS * 8 + field * 8, 8)
            work[pl.ds(base, 8), :] = x_change[number] + change[0, number, field]
        return carry

    lax.fori_loop(0, FIELDS, one_field, 0)

    for slot in range(SLOTS):
        for chunk in range(CHUNKS):
            base = (chunk // 2) * FIELDS * 8 + 2 * slot + chunk % 2
            cells = slice(chunk * LANES, (chunk + 1) * LANES)
            fresh = (
                state[0, 0, slot, :, cells]
                - courant * work[pl.ds(base, FIELDS, stride=8), :]
            )
            if slot == SLOTS - 1:
                moved[chunk * FIELDS : (chunk + 1) * FIELDS, :] = fresh
            out[0, 0, slot, :, cells] = jnp.where(slot < last_count, fresh, 0.0)


def update(state, planes, own_faces, low_faces, high_faces, links, counts, rounds):
    vmem = pl.BlockSpec(memory_space=pltpu.VMEM)
    smem = pl.BlockSpec(memory_space=pltpu.SMEM)
    return pl.pallas_call(
        functools.partial(update_kernel, rounds),
        out_shape=(
            jax.ShapeDtypeStruct(state.shape, jnp.float32),
            jax.ShapeDtypeStruct((CHUNKS * FIELDS, LANES), jnp.float32),
        ),
        in_specs=[vmem] * 5 + [smem] * 2,
        out_specs=(vmem, vmem),
        scratch_shapes=[
            pltpu.VMEM((6 * 2 * FIELDS * 8, LANES), jnp.float32),
            pltpu.VMEM((3, EDGE, FIELDS, 8, LANES), jnp.float32),
            pltpu.VMEM((EDGE * FIELDS * 8, LANES), jnp.float32),
        ],
        compiler_params=pltpu.CompilerParams(vmem_limit_bytes=VMEM_LIMIT),
        name="update",
    )(state, planes, own_faces, low_faces, high_faces, links, counts)


def place_kernel(rounds, *refs):
    arrived, (_, counts, out, block, sem) = refs[:rounds], refs[rounds:]
    sub_index = lax.axis_index("sub")
    start, _, arrival = final_counts(counts, sub_index, rounds)

    @pl.when(arrival >= 0)
    def _():
        for chunk in range(CHUNKS):
            rows = slice(chunk * FIELDS, (chunk + 1) * FIELDS)
            value = arrived[0][rows, :]
            for bit in range(1, rounds):
                value = jnp.where(arrival == bit, arrived[bit][rows, :], value)
            block[:, chunk * LANES : (chunk + 1) * LANES] = value
        copy = pltpu.make_async_copy(block, out.at[0, 0, start], sem)
        copy.start()
        copy.wait()


def place(arrived, out, counts):
    rounds = len(arrived)
    vmem = pl.BlockSpec(memory_space=pltpu.VMEM)
    smem = pl.BlockSpec(memory_space=pltpu.SMEM)
    anywhere = pl.BlockSpec(memory_space=pl.ANY)
    return pl.pallas_call(
        functools.partial(place_kernel, rounds),
        out_shape=jax.ShapeDtypeStruct(out.shape, out.dtype),
        in_specs=[vmem] * rounds + [anywhere, smem],
        out_specs=anywhere,
        scratch_shapes=[
            pltpu.VMEM((FIELDS, EDGE**3), jnp.float32),
            pltpu.SemaphoreType.DMA,
        ],
        input_output_aliases={rounds: 0},
        compiler_params=pltpu.CompilerParams(vmem_limit_bytes=VMEM_LIMIT),
        name="place",
    )(*arrived, out, counts)


def body(state, neighbours, counts):
    size = lax.axis_size("blocks")
    rounds = lax.axis_size("sub").bit_length() - 1
    planes, faces = prepare(state)
    forward = [(i, i + 1) for i in range(size - 1)]
    backward = [(i + 1, i) for i in range(size - 1)]
    low = lax.ppermute(faces, "blocks", forward)
    high = lax.ppermute(faces, "blocks", backward)
    out, moved = update(state, planes, faces, low, high, neighbours, counts, rounds)
    arrived = [
        lax.ppermute(
            moved, "sub", [(s, s ^ (1 << bit)) for s in range(lax.axis_size("sub"))]
        )
        for bit in range(rounds)
    ]
    return place(arrived, out, counts)


def solution(mesh):
    return jax.shard_map(
        body,
        mesh=mesh,
        in_specs=(
            P("blocks", "sub", None, None, None),
            P("blocks", "sub", None, None, None),
            P("blocks", None),
        ),
        out_specs=P("blocks", "sub", None, None, None),
        check_vma=False,
    )
```

```python
import functools

import jax
import jax.numpy as jnp
from jax import lax
from jax.experimental import pallas as pl
from jax.experimental.pallas import tpu as pltpu
from jax.sharding import PartitionSpec as P

EDGE = 16
FIELDS = 5
SLOTS = 3
LANES = 128
ROWS = 2 * SLOTS
BLOCK_ROWS = 2 * EDGE * FIELDS
FACE_ROWS = 6 * 2 * FIELDS * ROWS

heat_ratio = 1.4
courant = 0.07

VMEM_LIMIT = 48 * 1024 * 1024


def swap_chunks(planes, width, lane):
    planes = list(planes)
    step = 1
    while step < len(planes):
        upper = (lane & (step * width)) != 0
        for low in range(len(planes)):
            if low & step:
                continue
            a, b = planes[low], planes[low + step]
            planes[low] = jnp.where(upper, pltpu.roll(b, step * width, 1), a)
            planes[low + step] = jnp.where(upper, b, pltpu.roll(a, LANES - step * width, 1))
        step *= 2
    return planes


def swap_halves(planes, row):
    odd = (row & 1) != 0
    half = len(planes) // 2
    first = [jnp.where(odd, pltpu.roll(b, 1, 0), a) for a, b in zip(planes[:half], planes[half:])]
    second = [jnp.where(odd, b, pltpu.roll(a, 7, 0)) for a, b in zip(planes[:half], planes[half:])]
    return first + second


def tile_iotas():
    return (
        lax.broadcasted_iota(jnp.int32, (8, LANES), 1),
        lax.broadcasted_iota(jnp.int32, (8, LANES), 0),
    )


def x_to_y(planes, lane, row):
    planes = swap_chunks(planes[:8], EDGE, lane) + swap_chunks(planes[8:], EDGE, lane)
    return swap_halves(planes, row)


def y_to_x(planes, lane, row):
    planes = swap_halves(planes, row)
    return swap_chunks(planes[:8], EDGE, lane) + swap_chunks(planes[8:], EDGE, lane)


def row_moves():
    for slot in range(SLOTS):
        for field in range(FIELDS):
            for half in range(2):
                here = slot * BLOCK_ROWS + field * 2 * EDGE + half
                there = field * 8 + 2 * slot + half
                yield (
                    slot,
                    field,
                    half,
                    pl.ds(here, EDGE, stride=2),
                    pl.ds(there, EDGE, stride=FIELDS * 8),
                )


def prepare_kernel(state, planes, faces, work):
    for slot, field, half, here, there in row_moves():
        work[there, :] = state[here, :]
    for number in range(EDGE):
        base = number * FIELDS * 8
        rows = [work[base + 8 * field : base + 8 * field + 8, :] for field in range(FIELDS)]
        inverse = 1.0 / rows[0]
        v1, v2, v3 = rows[1] * inverse, rows[2] * inverse, rows[3] * inverse
        pressure = (heat_ratio - 1.0) * (
            rows[4] - 0.5 * rows[0] * (v1 * v1 + v2 * v2 + v3 * v3)
        )
        for field, value in enumerate((rows[0], v1, v2, v3, pressure)):
            planes[0, number, field] = value

    lane, row = tile_iotas()

    def one_field(field, carry):
        x_planes = [planes[0, number, field] for number in range(EDGE)]
        y_planes = x_to_y(x_planes, lane, row)
        for number in range(EDGE):
            planes[1, number, field] = y_planes[number]
        z_planes = swap_chunks(x_planes, 1, lane)
        for number in range(EDGE):
            planes[2, number, field] = z_planes[number]
        return carry

    lax.fori_loop(0, FIELDS, one_field, 0)

    for axis in range(3):
        for side in range(2):
            for depth in range(2):
                number = depth if side == 0 else EDGE - 1 - depth
                for field in range(FIELDS):
                    base = (((2 * axis + side) * 2 + depth) * FIELDS + field) * ROWS
                    faces[base : base + ROWS, :] = planes[axis, number, field, 0:ROWS, :]


def prepare(state):
    return pl.pallas_call(
        prepare_kernel,
        out_shape=(
            jax.ShapeDtypeStruct((3, EDGE, FIELDS, 8, LANES), jnp.float32),
            jax.ShapeDtypeStruct((FACE_ROWS, LANES), jnp.float32),
        ),
        scratch_shapes=[pltpu.VMEM((EDGE * FIELDS * 8, LANES), jnp.float32)],
        compiler_params=pltpu.CompilerParams(vmem_limit_bytes=VMEM_LIMIT),
        name="prepare",
    )(state)


def minmod(first, second):
    return jnp.maximum(jnp.minimum(first, second), 0.0) + jnp.minimum(
        jnp.maximum(first, second), 0.0
    )


def side_speeds(prim, component):
    scaled = heat_ratio * prim[4]
    sound = scaled * lax.rsqrt(scaled * prim[0])
    return prim[component] - sound, prim[component] + sound


def hll_flux(left, right, component):
    slow_left, fast_left = side_speeds(left, component)
    slow_right, fast_right = side_speeds(right, component)
    slow = jnp.minimum(jnp.minimum(slow_left, slow_right), 0.0)
    fast = jnp.maximum(jnp.maximum(fast_left, fast_right), 0.0)
    inverse = 1.0 / (fast - slow)
    weight_left = fast * inverse
    weight_right = -slow * inverse
    product = slow * weight_left
    normal_left, normal_right = left[component], right[component]
    carry_left = weight_left * normal_left - product
    carry_right = weight_right * normal_right + product
    mass_left, mass_right = carry_left * left[0], carry_right * right[0]
    push_left, push_right = weight_left * left[4], weight_right * right[4]
    outputs = [mass_left + mass_right]
    for number in (1, 2, 3):
        value = mass_left * left[number] + mass_right * right[number]
        if number == component:
            value = value + (push_left + push_right)
        outputs.append(value)
    square_left = left[1] * left[1] + left[2] * left[2] + left[3] * left[3]
    square_right = right[1] * right[1] + right[2] * right[2] + right[3] * right[3]
    inner = 1.0 / (heat_ratio - 1.0)
    energy = 0.5 * (mass_left * square_left + mass_right * square_right)
    energy = energy + inner * (carry_left * left[4] + carry_right * right[4])
    energy = energy + (push_left * normal_left + push_right * normal_right)
    outputs.append(energy)
    return outputs


def final_counts(counts, sub_index, rounds):
    size = counts.shape[-1]
    now = [counts[0, position] for position in range(size)]

    def own(values):
        picked = values[0]
        for position in range(1, size):
            picked = jnp.where(sub_index == position, values[position], picked)
        return picked

    start = own(now)
    arrival = jnp.int32(-1)
    for bit in range(rounds):
        gains = [
            jnp.maximum(now[p ^ (1 << bit)] - now[p], 0) // 2
            - jnp.maximum(now[p] - now[p ^ (1 << bit)], 0) // 2
            for p in range(size)
        ]
        arrival = jnp.where(own(gains) > 0, bit, arrival)
        now = [value + gain for value, gain in zip(now, gains)]
    return start, own(now), arrival


def update_kernel(
    rounds, state, planes, own_faces, high_faces, low_faces, links, counts, out, moved, ghosts, change, work
):
    sub_index = lax.axis_index("sub")
    _, last_count, _ = final_counts(counts, sub_index, rounds)

    for face in range(6):
        for slot in range(SLOTS):
            owner = links[0, 0, slot, face, 0]
            boundary = owner == 3
            source = jnp.where(boundary, slot, links[0, 0, slot, face, 1])
            side = jnp.where(boundary, face, face ^ 1)
            for half in range(2):
                base = side * (2 * FIELDS * ROWS) + 2 * source + half
                rows = pl.ds(base, 2 * FIELDS, stride=ROWS)
                values = jnp.where(
                    owner == 0,
                    low_faces[rows, :],
                    jnp.where(owner == 2, high_faces[rows, :], own_faces[rows, :]),
                )
                target = face * (2 * FIELDS * 8) + 2 * slot + half
                ghosts[pl.ds(target, 2 * FIELDS, stride=8), :] = values

    def cell(axis, number):
        if 0 <= number < EDGE:
            return [planes[axis, number, field] for field in range(FIELDS)]
        face = 2 * axis if number < 0 else 2 * axis + 1
        depth = -1 - number if number < 0 else number - EDGE
        base = face * (2 * FIELDS * 8) + depth * FIELDS * 8
        return [ghosts[base + 8 * field : base + 8 * field + 8, :] for field in range(FIELDS)]

    for axis in range(3):
        here = cell(axis, -1)
        diff = [b - a for a, b in zip(cell(axis, -2), here)]
        left, flux = None, None
        for number in range(-1, EDGE + 1):
            after = cell(axis, number + 1)
            next_diff = [b - a for a, b in zip(here, after)]
            half_slope = [0.5 * minmod(a, b) for a, b in zip(diff, next_diff)]
            if left is not None:
                right = [a - b for a, b in zip(here, half_slope)]
                next_flux = hll_flux(left, right, axis + 1)
                if flux is not None:
                    for field in range(FIELDS):
                        change[axis, number - 1, field] = next_flux[field] - flux[field]
                flux = next_flux
            left = [a + b for a, b in zip(here, half_slope)]
            here, diff = after, next_diff

    lane, row = tile_iotas()

    def one_field(field, carry):
        z_change = swap_chunks([change[2, number, field] for number in range(EDGE)], 1, lane)
        y_change = y_to_x([change[1, number, field] for number in range(EDGE)], lane, row)
        for number in range(EDGE):
            base = pl.multiple_of(number * FIELDS * 8 + field * 8, 8)
            work[pl.ds(base, 8), :] = (change[0, number, field] + y_change[number]) + z_change[number]
        return carry

    lax.fori_loop(0, FIELDS, one_field, 0)

    for slot, field, half, here, there in row_moves():
        fresh = state[here, :] - courant * work[there, :]
        if slot == SLOTS - 1:
            moved[pl.ds(field * 2 * EDGE + half, EDGE, stride=2), :] = fresh
        out[here, :] = jnp.where(slot < last_count, fresh, 0.0)


def update(state, planes, own_faces, high_faces, low_faces, links, counts, rounds):
    vmem = pl.BlockSpec(memory_space=pltpu.VMEM)
    smem = pl.BlockSpec(memory_space=pltpu.SMEM)
    return pl.pallas_call(
        functools.partial(update_kernel, rounds),
        out_shape=(
            jax.ShapeDtypeStruct(state.shape, jnp.float32),
            jax.ShapeDtypeStruct((BLOCK_ROWS, LANES), jnp.float32),
        ),
        in_specs=[vmem] * 5 + [smem] * 2,
        out_specs=(vmem, vmem),
        scratch_shapes=[
            pltpu.VMEM((6 * 2 * FIELDS * 8, LANES), jnp.float32),
            pltpu.VMEM((3, EDGE, FIELDS, 8, LANES), jnp.float32),
            pltpu.VMEM((EDGE * FIELDS * 8, LANES), jnp.float32),
        ],
        compiler_params=pltpu.CompilerParams(vmem_limit_bytes=VMEM_LIMIT),
        name="update",
    )(state, planes, own_faces, high_faces, low_faces, links, counts)


def place_kernel(rounds, *refs):
    arrived, (_, counts, out, sem) = refs[:rounds], refs[rounds:]
    sub_index = lax.axis_index("sub")
    _, _, arrival = final_counts(counts, sub_index, rounds)
    for bit in range(rounds):

        @pl.when(arrival == bit)
        def _():
            copy = pltpu.make_async_copy(arrived[bit], out.at[pl.ds(BLOCK_ROWS, BLOCK_ROWS)], sem)
            copy.start()
            copy.wait()


def place(arrived, out, counts):
    rounds = len(arrived)
    vmem = pl.BlockSpec(memory_space=pltpu.VMEM)
    smem = pl.BlockSpec(memory_space=pltpu.SMEM)
    anywhere = pl.BlockSpec(memory_space=pl.ANY)
    return pl.pallas_call(
        functools.partial(place_kernel, rounds),
        out_shape=jax.ShapeDtypeStruct(out.shape, out.dtype),
        in_specs=[vmem] * rounds + [anywhere, smem],
        out_specs=anywhere,
        scratch_shapes=[pltpu.SemaphoreType.DMA],
        input_output_aliases={rounds: 0},
        name="place",
    )(*arrived, out, counts)


def body(state, neighbours, counts):
    size = lax.axis_size("blocks")
    rounds = lax.axis_size("sub").bit_length() - 1
    shape = state.shape
    state = state.reshape(SLOTS * BLOCK_ROWS, LANES)
    planes, faces = prepare(state)
    forward = [(i, i + 1) for i in range(size - 1)]
    backward = [(i + 1, i) for i in range(size - 1)]
    high = lax.ppermute(faces, "blocks", backward)
    low = lax.ppermute(faces, "blocks", forward)
    out, moved = update(state, planes, faces, high, low, neighbours, counts, rounds)
    arrived = [
        lax.ppermute(
            moved, "sub", [(s, s ^ (1 << bit)) for s in range(lax.axis_size("sub"))]
        )
        for bit in range(rounds)
    ]
    return place(arrived, out, counts).reshape(shape)


def solution(mesh):
    return jax.shard_map(
        body,
        mesh=mesh,
        in_specs=(
            P("blocks", "sub", None, None, None),
            P("blocks", "sub", None, None, None),
            P("blocks", None),
        ),
        out_specs=P("blocks", "sub", None, None, None),
        check_vma=False,
    )
```

```python
import functools

import jax
import jax.numpy as jnp
from jax import lax
from jax.experimental import pallas as pl
from jax.experimental.pallas import tpu as pltpu
from jax.sharding import PartitionSpec as P

EDGE = 16
FIELDS = 5
SLOTS = 3
LANES = 128
BLOCK_ROWS = 2 * EDGE * FIELDS
FACE_ROWS = 3 * 4 * FIELDS * 8
OUTER = (0, 1, EDGE - 1, EDGE - 2)

heat_ratio = 1.4
courant = 0.07

VMEM_LIMIT = 16 * 1024 * 1024


def square_moves():
    for slot in range(SLOTS):
        for field in range(FIELDS):
            for half in range(2):
                here = pl.ds((slot * FIELDS + field) * 2 * EDGE + half, EDGE, stride=2)
                there = slice(half * 64 + slot * EDGE, half * 64 + (slot + 1) * EDGE)
                yield slot, field, half, here, there


def comb(number):
    return pl.ds(number, 8, stride=EDGE)


def band(number):
    return slice(number * EDGE, (number + 1) * EDGE)


def face_rows(axis, place, field):
    base = axis * 4 * FIELDS * 8
    if axis == 1:
        return slice(base + (field * 2 + place) * EDGE, base + (field * 2 + place + 1) * EDGE)
    return slice(base + (place * FIELDS + field) * 8, base + (place * FIELDS + field + 1) * 8)


def lanes_of(rows):
    return lax.broadcasted_iota(jnp.int32, (rows, LANES), 1)


def primitives(cells):
    inverse = 1.0 / cells[0]
    v1, v2, v3 = cells[1] * inverse, cells[2] * inverse, cells[3] * inverse
    square = v1 * v1 + v2 * v2 + v3 * v3
    pressure = (heat_ratio - 1.0) * (cells[4] - 0.5 * cells[0] * square)
    return cells[0], v1, v2, v3, pressure


def prepare_kernel(state, upright, turned, faces):
    for half in range(2):
        for slot in range(SLOTS):
            cells = [
                state[pl.ds((slot * FIELDS + field) * 2 * EDGE + half, EDGE, stride=2), :]
                for field in range(FIELDS)
            ]
            for field, value in enumerate(primitives(cells)):
                upright[field, band(4 * half + slot), :] = value
                if slot == SLOTS - 1:
                    upright[field, band(4 * half + slot + 1), :] = value
    low_half = lanes_of(EDGE) < 64
    for field in range(FIELDS):
        turned[field] = upright[field].T
    for field in range(FIELDS):
        for place, number in enumerate(OUTER):
            faces[face_rows(0, place, field), :] = upright[field, comb(number), :]
            faces[face_rows(2, place, field), :] = turned[field, comb(number), :]
        for depth in range(2):
            faces[face_rows(1, depth, field), :] = jnp.where(
                low_half, turned[field, band(depth), :], turned[field, band(7 - depth), :]
            )


SQUARES = jax.ShapeDtypeStruct((FIELDS, LANES, LANES), jnp.float32)


def prepare(state):
    return pl.pallas_call(
        prepare_kernel,
        out_shape=(SQUARES, SQUARES, jax.ShapeDtypeStruct((FACE_ROWS, LANES), jnp.float32)),
        compiler_params=pltpu.CompilerParams(vmem_limit_bytes=VMEM_LIMIT),
        name="prepare",
    )(state)


def minmod(first, second):
    return jnp.maximum(jnp.minimum(first, second), 0.0) + jnp.minimum(
        jnp.maximum(first, second), 0.0
    )


def side_speeds(prim, component):
    scaled = heat_ratio * prim[4]
    sound = scaled * lax.rsqrt(scaled * prim[0])
    return prim[component] - sound, prim[component] + sound


def hll_flux(left, right, component):
    slow_left, fast_left = side_speeds(left, component)
    slow_right, fast_right = side_speeds(right, component)
    slow = jnp.minimum(jnp.minimum(slow_left, slow_right), 0.0)
    fast = jnp.maximum(jnp.maximum(fast_left, fast_right), 0.0)
    inverse = 1.0 / (fast - slow)
    weight_left = fast * inverse
    weight_right = -slow * inverse
    product = slow * weight_left
    normal_left, normal_right = left[component], right[component]
    carry_left = weight_left * normal_left - product
    carry_right = weight_right * normal_right + product
    mass_left, mass_right = carry_left * left[0], carry_right * right[0]
    push_left, push_right = weight_left * left[4], weight_right * right[4]
    outputs = [mass_left + mass_right]
    for number in (1, 2, 3):
        value = mass_left * left[number] + mass_right * right[number]
        if number == component:
            value = value + (push_left + push_right)
        outputs.append(value)
    square_left = left[1] * left[1] + left[2] * left[2] + left[3] * left[3]
    square_right = right[1] * right[1] + right[2] * right[2] + right[3] * right[3]
    inner = 1.0 / (heat_ratio - 1.0)
    energy = 0.5 * (mass_left * square_left + mass_right * square_right)
    energy = energy + inner * (carry_left * left[4] + carry_right * right[4])
    energy = energy + (push_left * normal_left + push_right * normal_right)
    outputs.append(energy)
    return outputs


def half_slopes(before, here, after):
    return [0.5 * minmod(b - a, c - b) for a, b, c in zip(before, here, after)]


def add(first, second):
    return [a + b for a, b in zip(first, second)]


def sub(first, second):
    return [a - b for a, b in zip(first, second)]


GROUPS = 5


def ghost_codes(links, codes):
    lane = lanes_of(EDGE)
    row = lax.broadcasted_iota(jnp.int32, (EDGE, LANES), 0)

    def by_slot(slot, face, part):
        last = links[2, part, face]
        return jnp.where(slot == 0, links[0, part, face], jnp.where(slot == 1, links[1, part, face], last))

    for side in range(2):
        slot = row & 3
        codes[side, 0] = by_slot(slot, side, 0)
        codes[side, 1] = (row & 4) + by_slot(slot, side, 1)
    slot = (lane >> 4) & 3
    inside = lane & (EDGE - 1)
    low_half = lane < 64
    for part in range(2):
        value = jnp.where(low_half, by_slot(slot, 2, part), by_slot(slot, 3, part))
        if part == 1:
            value = 64 - (lane & 64) + value * EDGE + inside
        codes[2, part] = value
    for side in range(2):
        codes[3 + side, 0] = by_slot(slot, 4 + side, 0)
        codes[3 + side, 1] = (lane & 64) + by_slot(slot, 4 + side, 1) * EDGE + inside


def inner_line(cell, size, component, store):
    before, here = cell(0), cell(1)
    left, flux = None, None
    for number in range(1, size - 1):
        after = cell(number + 1)
        slopes = half_slopes(before, here, after)
        if left is not None:
            next_flux = hll_flux(left, sub(here, slopes), component)
            store(number - 1, next_flux if flux is None else sub(next_flux, flux))
            flux = next_flux
        left = add(here, slopes)
        before, here = here, after
    store(size - 2, [-value for value in flux])


def inner_kernel(upright, turned, links, up_change, turned_change, codes):
    def store_comb(change):
        def store(number, values):
            for field in range(FIELDS):
                change[field, comb(number), :] = values[field]

        return store

    def add_band(number, values):
        for field in range(FIELDS):
            turned_change[field, band(number), :] += values[field]

    nothing = [jnp.zeros((8, LANES), jnp.float32)] * FIELDS
    for change in (up_change, turned_change):
        for number in (0, EDGE - 1):
            store_comb(change)(number, nothing)
    inner_line(
        lambda number: [upright[field, comb(number), :] for field in range(FIELDS)],
        EDGE,
        1,
        store_comb(up_change),
    )
    inner_line(
        lambda number: [turned[field, comb(number), :] for field in range(FIELDS)],
        EDGE,
        3,
        store_comb(turned_change),
    )
    inner_line(
        lambda number: [turned[field, band(number), :] for field in range(FIELDS)],
        8,
        2,
        add_band,
    )
    ghost_codes(links, codes)


def interior(upright, turned, links):
    vmem = pl.BlockSpec(memory_space=pltpu.VMEM)
    return pl.pallas_call(
        inner_kernel,
        out_shape=(
            SQUARES,
            SQUARES,
            jax.ShapeDtypeStruct((GROUPS, 2, EDGE, LANES), jnp.int32),
        ),
        in_specs=[vmem, vmem, pl.BlockSpec(memory_space=pltpu.SMEM)],
        out_specs=(vmem,) * 3,
        compiler_params=pltpu.CompilerParams(vmem_limit_bytes=VMEM_LIMIT),
        cost_estimate=pl.CostEstimate(flops=6_000_000, bytes_accessed=3_000_000, transcendentals=0),
        name="interior",
    )(upright, turned, links)


def final_counts(counts, sub_index, rounds):
    size = counts.shape[-1]
    now = [counts[0, position] for position in range(size)]

    def own(values):
        picked = values[0]
        for position in range(1, size):
            picked = jnp.where(sub_index == position, values[position], picked)
        return picked

    start = own(now)
    arrival = jnp.int32(-1)
    for bit in range(rounds):
        gains = [
            jnp.maximum(now[p ^ (1 << bit)] - now[p], 0) // 2
            - jnp.maximum(now[p] - now[p ^ (1 << bit)], 0) // 2
            for p in range(size)
        ]
        arrival = jnp.where(own(gains) > 0, bit, arrival)
        now = [value + gain for value, gain in zip(now, gains)]
    return start, own(now), arrival


def outer_side(near, far, first, second, third, side, component):
    slopes = half_slopes(near, first, second)
    if side == 0:
        beyond = add(near, half_slopes(far, near, first))
        within = sub(second, half_slopes(first, second, third))
        outside = hll_flux(beyond, sub(first, slopes), component)
        inside = hll_flux(add(first, slopes), within, component)
        return sub(inside, outside), [-value for value in inside]
    slopes = half_slopes(second, first, near)
    beyond = sub(near, half_slopes(first, near, far))
    within = add(second, half_slopes(third, second, first))
    outside = hll_flux(add(first, slopes), beyond, component)
    inside = hll_flux(within, sub(first, slopes), component)
    return sub(outside, inside), inside


def outer_kernel(
    state,
    upright,
    turned,
    up_change,
    turned_change,
    codes,
    own_faces,
    high_faces,
    low_faces,
    total,
    moved,
    fixed,
):
    def ghost(group, axis, place, mirror, field):
        rows = 8 if axis != 1 else EDGE
        owner, source = codes[group, 0, 0:rows, :], codes[group, 1, 0:rows, :]
        there = face_rows(axis, mirror, field)
        low, own, high = (
            jnp.take_along_axis(faces[there, :], source, axis=0 if axis == 0 else 1)
            for faces in (low_faces, own_faces, high_faces)
        )
        neighbour = jnp.where(owner == 0, low, jnp.where(owner == 1, own, high))
        return jnp.where(owner == 3, own_faces[face_rows(axis, place, field), :], neighbour)

    low_half = lanes_of(EDGE) < 64
    for field in range(FIELDS):
        fixed[field] = turned_change[field]

    cells = {
        number: [turned[field, band(number), :] for field in range(FIELDS)]
        for number in (0, 1, 2, 5, 6, 7)
    }
    ghosts = [[ghost(2, 1, depth, depth, field) for field in range(FIELDS)] for depth in range(2)]
    for side in range(2):
        numbers = (0, 1, 2) if side == 0 else (7, 6, 5)
        outside = []
        for depth in range(2):
            other = cells[7 - depth if side == 0 else depth]
            across = [pltpu.roll(value, 64, 1) for value in other]
            pair = (ghosts[depth], across) if side == 0 else (across, ghosts[depth])
            outside.append([jnp.where(low_half, a, b) for a, b in zip(*pair)])
        parts = outer_side(*outside, *(cells[number] for number in numbers), side, 2)
        for number, part in zip(numbers, parts):
            for field in range(FIELDS):
                fixed[field, band(number), :] += part[field]

    def comb_sides(square, axis, group, change):
        for side in range(2):
            numbers = (0, 1, 2) if side == 0 else (EDGE - 1, EDGE - 2, EDGE - 3)
            planes = [
                [square[field, comb(number), :] for field in range(FIELDS)] for number in numbers
            ]
            outside = [
                [
                    ghost(group + side, axis, 2 * side + depth, 2 * (1 - side) + depth, field)
                    for field in range(FIELDS)
                ]
                for depth in range(2)
            ]
            parts = outer_side(*outside, *planes, side, axis + 1)
            for number, part in zip(numbers, parts):
                for field in range(FIELDS):
                    change[field, comb(number), :] += part[field]

    comb_sides(turned, 2, 3, fixed)
    for field in range(FIELDS):
        total[field] = up_change[field] + fixed[field].T
    comb_sides(upright, 0, 0, total)

    for slot, field, half, here, there in square_moves():
        if slot == SLOTS - 1:
            moved[pl.ds(field * 2 * EDGE + half, EDGE, stride=2), :] = (
                state[here, :] - courant * total[field, there, :]
            )


def outer(*operands):
    vmem = pl.BlockSpec(memory_space=pltpu.VMEM)
    return pl.pallas_call(
        outer_kernel,
        out_shape=(SQUARES, jax.ShapeDtypeStruct((BLOCK_ROWS, LANES), jnp.float32)),
        in_specs=[vmem] * len(operands),
        out_specs=(vmem, vmem),
        scratch_shapes=[pltpu.VMEM(SQUARES.shape, jnp.float32)],
        compiler_params=pltpu.CompilerParams(vmem_limit_bytes=VMEM_LIMIT),
        name="outer",
    )(*operands)


def finish_kernel(rounds, state, total, counts, out):
    _, last_count, _ = final_counts(counts, lax.axis_index("sub"), rounds)
    for slot, field, _, here, there in square_moves():
        fresh = state[here, :] - courant * total[field, there, :]
        out[here, :] = jnp.where(slot < last_count, fresh, 0.0)


def finish(state, total, counts, rounds):
    vmem = pl.BlockSpec(memory_space=pltpu.VMEM)
    smem = pl.BlockSpec(memory_space=pltpu.SMEM)
    return pl.pallas_call(
        functools.partial(finish_kernel, rounds),
        out_shape=jax.ShapeDtypeStruct(state.shape, jnp.float32),
        in_specs=[vmem, vmem, smem],
        out_specs=vmem,
        compiler_params=pltpu.CompilerParams(vmem_limit_bytes=VMEM_LIMIT),
        cost_estimate=pl.CostEstimate(flops=200_000, bytes_accessed=1_000_000, transcendentals=0),
        name="finish",
    )(state, total, counts)


def place_kernel(rounds, *refs):
    arrived, (_, counts, out, sem) = refs[:rounds], refs[rounds:]
    sub_index = lax.axis_index("sub")
    _, _, arrival = final_counts(counts, sub_index, rounds)
    for bit in range(rounds):

        @pl.when(arrival == bit)
        def _():
            copy = pltpu.make_async_copy(arrived[bit], out.at[pl.ds(BLOCK_ROWS, BLOCK_ROWS)], sem)
            copy.start()
            copy.wait()


def place(arrived, out, counts):
    rounds = len(arrived)
    vmem = pl.BlockSpec(memory_space=pltpu.VMEM)
    smem = pl.BlockSpec(memory_space=pltpu.SMEM)
    anywhere = pl.BlockSpec(memory_space=pl.ANY)
    return pl.pallas_call(
        functools.partial(place_kernel, rounds),
        out_shape=jax.ShapeDtypeStruct(out.shape, out.dtype),
        in_specs=[vmem] * rounds + [anywhere, smem],
        out_specs=anywhere,
        scratch_shapes=[pltpu.SemaphoreType.DMA],
        input_output_aliases={rounds: 0},
        compiler_params=pltpu.CompilerParams(vmem_limit_bytes=1024 * 1024),
        name="place",
    )(*arrived, out, counts)


def body(state, neighbours, counts):
    size = lax.axis_size("blocks")
    rounds = lax.axis_size("sub").bit_length() - 1
    shape = state.shape
    state = state.reshape(SLOTS * BLOCK_ROWS, LANES)
    links = jnp.transpose(neighbours.reshape(SLOTS, 6, 2), (0, 2, 1))
    upright, turned, faces = prepare(state)
    forward = [(i, i + 1) for i in range(size - 1)]
    backward = [(i + 1, i) for i in range(size - 1)]
    high = lax.ppermute(faces, "blocks", backward)
    low = lax.ppermute(faces, "blocks", forward)
    changes = interior(upright, turned, links)
    total, moved = outer(state, upright, turned, *changes, faces, high, low)
    arrived = [
        lax.ppermute(
            moved, "sub", [(s, s ^ (1 << bit)) for s in range(lax.axis_size("sub"))]
        )
        for bit in range(rounds)
    ]
    out = finish(state, total, counts, rounds)
    return place(arrived, out, counts).reshape(shape)


def solution(mesh):
    return jax.shard_map(
        body,
        mesh=mesh,
        in_specs=(
            P("blocks", "sub", None, None, None),
            P("blocks", "sub", None, None, None),
            P("blocks", None),
        ),
        out_specs=P("blocks", "sub", None, None, None),
        check_vma=False,
    )
```

```python
import functools

import jax
import jax.numpy as jnp
from jax import lax
from jax.experimental import pallas as pl
from jax.experimental.pallas import tpu as pltpu
from jax.sharding import PartitionSpec as P

EDGE = 16
FIELDS = 5
SLOTS = 3
LANES = 128
BLOCK_ROWS = 2 * EDGE * FIELDS
OUTER = (0, 1, EDGE - 1, EDGE - 2)

ROW = 16
RELAY = 5

heat_ratio = 1.4
courant = 0.07

VMEM_LIMIT = 16 * 1024 * 1024


def square_moves():
    for slot in range(SLOTS):
        for field in range(FIELDS):
            for half in range(2):
                here = pl.ds((slot * FIELDS + field) * 2 * EDGE + half, EDGE, stride=2)
                there = slice(half * 64 + slot * EDGE, half * 64 + (slot + 1) * EDGE)
                yield slot, field, half, here, there


def comb(number):
    return pl.ds(number, 8, stride=EDGE)


def band(number):
    return slice(number * EDGE, (number + 1) * EDGE)


def face_planes(axis):
    return [(field, place) for field in range(FIELDS) for place in range(2 if axis == 1 else 4)]


def carried(axis, number):
    return number % 4 == 3


def face_rows(axis, number):
    size = EDGE if axis == 1 else 8
    base = (0, 15 * 8, 15 * 8 + 8 * EDGE)[axis] + (number - number // 4) * size
    return slice(base, base + size)


FACE_ROWS = 15 * 8 + 8 * EDGE + 15 * 8


def face_plane(upright, turned, axis, field, place):
    if axis == 0:
        return upright[field, comb(OUTER[place]), :]
    if axis == 2:
        return turned[field, comb(OUTER[place]), :]
    return jnp.where(lanes_of(EDGE) < 64, turned[field, band(place), :], turned[field, band(7 - place), :])


def fourth_slot(axis):
    if axis == 0:
        return (lax.broadcasted_iota(jnp.int32, (8, LANES), 0) & 3) == 3
    return ((lanes_of(EDGE if axis == 1 else 8) >> 4) & 3) == 3


def lanes_of(rows):
    return lax.broadcasted_iota(jnp.int32, (rows, LANES), 1)


def primitives(cells):
    inverse = 1.0 / cells[0]
    v1, v2, v3 = cells[1] * inverse, cells[2] * inverse, cells[3] * inverse
    square = v1 * v1 + v2 * v2 + v3 * v3
    pressure = (heat_ratio - 1.0) * (cells[4] - 0.5 * cells[0] * square)
    return cells[0], v1, v2, v3, pressure


def prepare_kernel(state, upright, turned, faces):
    for half in range(2):
        for slot in range(SLOTS):
            cells = [
                state[pl.ds((slot * FIELDS + field) * 2 * EDGE + half, EDGE, stride=2), :]
                for field in range(FIELDS)
            ]
            for field, value in enumerate(primitives(cells)):
                upright[field, band(4 * half + slot), :] = value
                if slot == SLOTS - 1:
                    upright[field, band(4 * half + slot + 1), :] = value
    for field in range(FIELDS):
        turned[field] = upright[field].T
    for axis in range(3):
        planes = face_planes(axis)
        fourth = fourth_slot(axis)
        for number, (field, place) in enumerate(planes):
            if carried(axis, number):
                continue
            value = face_plane(upright, turned, axis, field, place)
            rider = number | 3
            if rider < len(planes):
                other = face_plane(upright, turned, axis, *planes[rider])
                shift = 3 - number % 4
                other = pltpu.roll(other, shift, 0) if axis == 0 else pltpu.roll(other, shift * EDGE, 1)
                value = jnp.where(fourth, other, value)
            faces[face_rows(axis, number), :] = value


SQUARES = jax.ShapeDtypeStruct((FIELDS, LANES, LANES), jnp.float32)


def prepare(state):
    return pl.pallas_call(
        prepare_kernel,
        out_shape=(SQUARES, SQUARES, jax.ShapeDtypeStruct((FACE_ROWS, LANES), jnp.float32)),
        compiler_params=pltpu.CompilerParams(vmem_limit_bytes=VMEM_LIMIT),
        name="prepare",
    )(state)


def minmod(first, second):
    return jnp.maximum(jnp.minimum(first, second), 0.0) + jnp.minimum(
        jnp.maximum(first, second), 0.0
    )


def side_speeds(prim, component):
    scaled = heat_ratio * prim[4]
    sound = scaled * lax.rsqrt(scaled * prim[0])
    return prim[component] - sound, prim[component] + sound


def hll_flux(left, right, component):
    slow_left, fast_left = side_speeds(left, component)
    slow_right, fast_right = side_speeds(right, component)
    slow = jnp.minimum(jnp.minimum(slow_left, slow_right), 0.0)
    fast = jnp.maximum(jnp.maximum(fast_left, fast_right), 0.0)
    inverse = 1.0 / (fast - slow)
    weight_left = fast * inverse
    weight_right = -slow * inverse
    product = slow * weight_left
    normal_left, normal_right = left[component], right[component]
    carry_left = weight_left * normal_left - product
    carry_right = weight_right * normal_right + product
    mass_left, mass_right = carry_left * left[0], carry_right * right[0]
    push_left, push_right = weight_left * left[4], weight_right * right[4]
    outputs = [mass_left + mass_right]
    for number in (1, 2, 3):
        value = mass_left * left[number] + mass_right * right[number]
        if number == component:
            value = value + (push_left + push_right)
        outputs.append(value)
    square_left = left[1] * left[1] + left[2] * left[2] + left[3] * left[3]
    square_right = right[1] * right[1] + right[2] * right[2] + right[3] * right[3]
    inner = 1.0 / (heat_ratio - 1.0)
    energy = 0.5 * (mass_left * square_left + mass_right * square_right)
    energy = energy + inner * (carry_left * left[4] + carry_right * right[4])
    energy = energy + (push_left * normal_left + push_right * normal_right)
    outputs.append(energy)
    return outputs


def half_slopes(before, here, after):
    return [0.5 * minmod(b - a, c - b) for a, b, c in zip(before, here, after)]


def add(first, second):
    return [a + b for a, b in zip(first, second)]


def sub(first, second):
    return [a - b for a, b in zip(first, second)]


GROUPS = 5


def ghost_codes(links, codes):
    lane = lanes_of(EDGE)
    row = lax.broadcasted_iota(jnp.int32, (EDGE, LANES), 0)

    def by_slot(slot, face, part):
        last = links[2, part, face]
        return jnp.where(slot == 0, links[0, part, face], jnp.where(slot == 1, links[1, part, face], last))

    for side in range(2):
        slot = row & 3
        codes[side, 0] = by_slot(slot, side, 0)
        codes[side, 1] = (row & 4) + by_slot(slot, side, 1)
    slot = (lane >> 4) & 3
    inside = lane & (EDGE - 1)
    low_half = lane < 64
    for part in range(2):
        value = jnp.where(low_half, by_slot(slot, 2, part), by_slot(slot, 3, part))
        if part == 1:
            value = 64 - (lane & 64) + value * EDGE + inside
        codes[2, part] = value
    for side in range(2):
        codes[3 + side, 0] = by_slot(slot, 4 + side, 0)
        codes[3 + side, 1] = (lane & 64) + by_slot(slot, 4 + side, 1) * EDGE + inside


def inner_line(cell, size, component, store):
    before, here = cell(0), cell(1)
    left, flux = None, None
    for number in range(1, size - 1):
        after = cell(number + 1)
        slopes = half_slopes(before, here, after)
        if left is not None:
            next_flux = hll_flux(left, sub(here, slopes), component)
            store(number - 1, next_flux if flux is None else sub(next_flux, flux))
            flux = next_flux
        left = add(here, slopes)
        before, here = here, after
    store(size - 2, [-value for value in flux])


def inner_kernel(upright, turned, links, up_change, turned_change, codes):
    def store_comb(change):
        def store(number, values):
            for field in range(FIELDS):
                change[field, comb(number), :] = values[field]

        return store

    def add_band(number, values):
        for field in range(FIELDS):
            turned_change[field, band(number), :] += values[field]

    nothing = [jnp.zeros((8, LANES), jnp.float32)] * FIELDS
    for change in (up_change, turned_change):
        for number in (0, EDGE - 1):
            store_comb(change)(number, nothing)
    inner_line(
        lambda number: [upright[field, comb(number), :] for field in range(FIELDS)],
        EDGE,
        1,
        store_comb(up_change),
    )
    inner_line(
        lambda number: [turned[field, comb(number), :] for field in range(FIELDS)],
        EDGE,
        3,
        store_comb(turned_change),
    )
    inner_line(
        lambda number: [turned[field, band(number), :] for field in range(FIELDS)],
        8,
        2,
        add_band,
    )
    ghost_codes(links, codes)


def interior(upright, turned, links):
    vmem = pl.BlockSpec(memory_space=pltpu.VMEM)
    return pl.pallas_call(
        inner_kernel,
        out_shape=(
            SQUARES,
            SQUARES,
            jax.ShapeDtypeStruct((GROUPS, 2, EDGE, LANES), jnp.int32),
        ),
        in_specs=[vmem, vmem, pl.BlockSpec(memory_space=pltpu.SMEM)],
        out_specs=(vmem,) * 3,
        compiler_params=pltpu.CompilerParams(vmem_limit_bytes=VMEM_LIMIT),
        cost_estimate=pl.CostEstimate(flops=6_000_000, bytes_accessed=3_000_000, transcendentals=0),
        name="interior",
    )(upright, turned, links)


def final_counts(counts, sub_index, rounds):
    size = counts.shape[-1]
    now = [counts[0, position] for position in range(size)]

    def own(values):
        picked = values[0]
        for position in range(1, size):
            picked = jnp.where(sub_index == position, values[position], picked)
        return picked

    start = own(now)
    arrival = jnp.int32(-1)
    for bit in range(rounds):
        gains = [
            jnp.maximum(now[p ^ (1 << bit)] - now[p], 0) // 2
            - jnp.maximum(now[p] - now[p ^ (1 << bit)], 0) // 2
            for p in range(size)
        ]
        arrival = jnp.where(own(gains) > 0, bit, arrival)
        now = [value + gain for value, gain in zip(now, gains)]
    return start, own(now), arrival


def outer_side(near, far, first, second, third, side, component):
    slopes = half_slopes(near, first, second)
    if side == 0:
        beyond = add(near, half_slopes(far, near, first))
        within = sub(second, half_slopes(first, second, third))
        outside = hll_flux(beyond, sub(first, slopes), component)
        inside = hll_flux(add(first, slopes), within, component)
        return sub(inside, outside), [-value for value in inside]
    slopes = half_slopes(second, first, near)
    beyond = sub(near, half_slopes(first, near, far))
    within = add(second, half_slopes(third, second, first))
    outside = hll_flux(add(first, slopes), beyond, component)
    inside = hll_flux(within, sub(first, slopes), component)
    return sub(outside, inside), inside


def outer_kernel(
    state,
    upright,
    turned,
    up_change,
    turned_change,
    codes,
    own_faces,
    high_crossing,
    high_faces,
    low_faces,
    total,
    moved,
    fixed,
):
    def ghost(group, axis, place, mirror, field):
        rows = 8 if axis != 1 else EDGE
        owner, source = codes[group, 0, 0:rows, :], codes[group, 1, 0:rows, :]
        number = face_planes(axis).index((field, mirror))

        def fetch(stored, index):
            there = face_rows(axis, stored)
            above = high_faces[there, :] + high_crossing[there, :]
            low, own, high = (
                jnp.take_along_axis(values, index, axis=0 if axis == 0 else 1)
                for values in (low_faces[there, :], own_faces[there, :], above)
            )
            return jnp.where(owner == 0, low, jnp.where(owner == 1, own, high))

        if carried(axis, number):
            slot = source & 3 if axis == 0 else (source >> 4) & 3
            index = source | (3 if axis == 0 else 3 * EDGE)
            first, second, third = (fetch(number - 3 + carrier, index) for carrier in range(3))
            neighbour = jnp.where(slot == 0, first, jnp.where(slot == 1, second, third))
        else:
            neighbour = fetch(number, source)
        return jnp.where(owner == 3, face_plane(upright, turned, axis, field, place), neighbour)

    low_half = lanes_of(EDGE) < 64
    for field in range(FIELDS):
        fixed[field] = turned_change[field]

    cells = {
        number: [turned[field, band(number), :] for field in range(FIELDS)]
        for number in (0, 1, 2, 5, 6, 7)
    }
    ghosts = [[ghost(2, 1, depth, depth, field) for field in range(FIELDS)] for depth in range(2)]
    for side in range(2):
        numbers = (0, 1, 2) if side == 0 else (7, 6, 5)
        outside = []
        for depth in range(2):
            other = cells[7 - depth if side == 0 else depth]
            across = [pltpu.roll(value, 64, 1) for value in other]
            pair = (ghosts[depth], across) if side == 0 else (across, ghosts[depth])
            outside.append([jnp.where(low_half, a, b) for a, b in zip(*pair)])
        parts = outer_side(*outside, *(cells[number] for number in numbers), side, 2)
        for number, part in zip(numbers, parts):
            for field in range(FIELDS):
                fixed[field, band(number), :] += part[field]

    def comb_sides(square, axis, group, change):
        for side in range(2):
            numbers = (0, 1, 2) if side == 0 else (EDGE - 1, EDGE - 2, EDGE - 3)
            planes = [
                [square[field, comb(number), :] for field in range(FIELDS)] for number in numbers
            ]
            outside = [
                [
                    ghost(group + side, axis, 2 * side + depth, 2 * (1 - side) + depth, field)
                    for field in range(FIELDS)
                ]
                for depth in range(2)
            ]
            parts = outer_side(*outside, *planes, side, axis + 1)
            for number, part in zip(numbers, parts):
                for field in range(FIELDS):
                    change[field, comb(number), :] += part[field]

    comb_sides(turned, 2, 3, fixed)
    for field in range(FIELDS):
        total[field] = up_change[field] + fixed[field].T
    comb_sides(upright, 0, 0, total)

    for slot, field, half, here, there in square_moves():
        if slot == SLOTS - 1:
            moved[pl.ds(field * 2 * EDGE + half, EDGE, stride=2), :] = (
                state[here, :] - courant * total[field, there, :]
            )


def outer(*operands):
    vmem = pl.BlockSpec(memory_space=pltpu.VMEM)
    return pl.pallas_call(
        outer_kernel,
        out_shape=(SQUARES, jax.ShapeDtypeStruct((BLOCK_ROWS, LANES), jnp.float32)),
        in_specs=[vmem] * len(operands),
        out_specs=(vmem, vmem),
        scratch_shapes=[pltpu.VMEM(SQUARES.shape, jnp.float32)],
        compiler_params=pltpu.CompilerParams(vmem_limit_bytes=VMEM_LIMIT),
        name="outer",
    )(*operands)


def finish_kernel(rounds, state, total, counts, out, second, arrival):
    _, last_count, arrival_round = final_counts(counts, lax.axis_index("sub"), rounds)
    arrival[...] = jnp.full(arrival.shape, arrival_round, jnp.int32)
    for slot, field, half, here, there in square_moves():
        fresh = state[here, :] - courant * total[field, there, :]
        fresh = jnp.where(slot < last_count, fresh, 0.0)
        out[here, :] = fresh
        if slot == 1:
            second[pl.ds(field * 2 * EDGE + half, EDGE, stride=2), :] = fresh


def finish(state, total, counts, rounds):
    vmem = pl.BlockSpec(memory_space=pltpu.VMEM)
    smem = pl.BlockSpec(memory_space=pltpu.SMEM)
    return pl.pallas_call(
        functools.partial(finish_kernel, rounds),
        out_shape=(
            jax.ShapeDtypeStruct(state.shape, jnp.float32),
            jax.ShapeDtypeStruct((BLOCK_ROWS, LANES), jnp.float32),
            jax.ShapeDtypeStruct((8, LANES), jnp.int32),
        ),
        in_specs=[vmem, vmem, smem],
        out_specs=(vmem,) * 3,
        compiler_params=pltpu.CompilerParams(vmem_limit_bytes=VMEM_LIMIT),
        cost_estimate=pl.CostEstimate(flops=200_000, bytes_accessed=1_000_000, transcendentals=0),
        name="finish",
    )(state, total, counts)


def place_kernel(rounds, *refs):
    arrived, (second, arrival, _, out, block, sem) = refs[:rounds], refs[rounds:]
    arrival_round = arrival[...]
    for row in range(0, BLOCK_ROWS, 8):
        rows = slice(row, row + 8)
        value = second[rows, :]
        for bit in range(rounds):
            value = jnp.where(arrival_round == bit, arrived[bit][rows, :], value)
        block[rows, :] = value
    copy = pltpu.make_async_copy(block, out.at[pl.ds(BLOCK_ROWS, BLOCK_ROWS)], sem)
    copy.start()
    copy.wait()


def place(arrived, out, second, arrival):
    rounds = len(arrived)
    vmem = pl.BlockSpec(memory_space=pltpu.VMEM)
    anywhere = pl.BlockSpec(memory_space=pl.ANY)
    return pl.pallas_call(
        functools.partial(place_kernel, rounds),
        out_shape=jax.ShapeDtypeStruct(out.shape, out.dtype),
        in_specs=[vmem] * (rounds + 2) + [anywhere],
        out_specs=anywhere,
        scratch_shapes=[
            pltpu.VMEM((BLOCK_ROWS, LANES), jnp.float32),
            pltpu.SemaphoreType.DMA,
        ],
        input_output_aliases={rounds + 2: 0},
        compiler_params=pltpu.CompilerParams(vmem_limit_bytes=1024 * 1024),
        name="place",
    )(*arrived, second, arrival, out)


def body(state, neighbours, counts):
    size = lax.axis_size("blocks")
    rounds = lax.axis_size("sub").bit_length() - 1
    shape = state.shape
    state = state.reshape(SLOTS * BLOCK_ROWS, LANES)
    links = jnp.transpose(neighbours.reshape(SLOTS, 6, 2), (0, 2, 1))
    upright, turned, faces = prepare(state)
    forward = [(i, i + 1) for i in range(size - 1)]
    firsts = range(ROW, size, ROW)
    backward = [(i + 1, i) for i in range(size - 1) if i + 1 not in firsts]
    low = lax.ppermute(faces, "blocks", forward)
    high = lax.ppermute(faces, "blocks", backward)
    changes = interior(upright, turned, links)
    relayed = lax.ppermute(faces, "blocks", [(i, i - ROW + RELAY) for i in firsts])
    crossing = lax.ppermute(relayed, "blocks", [(i - ROW + RELAY, i - 1) for i in firsts])
    total, moved = outer(state, upright, turned, *changes, faces, crossing, high, low)
    arrived = [
        lax.ppermute(
            moved, "sub", [(s, s ^ (1 << bit)) for s in range(lax.axis_size("sub"))]
        )
        for bit in range(rounds)
    ]
    out, second, arrival = finish(state, total, counts, rounds)
    return place(arrived, out, second, arrival).reshape(shape)


def solution(mesh):
    return jax.shard_map(
        body,
        mesh=mesh,
        in_specs=(
            P("blocks", "sub", None, None, None),
            P("blocks", "sub", None, None, None),
            P("blocks", None),
        ),
        out_specs=P("blocks", "sub", None, None, None),
        check_vma=False,
    )
```

```python
import functools

import jax
import jax.numpy as jnp
from jax import lax
from jax.experimental import pallas as pl
from jax.experimental.pallas import tpu as pltpu
from jax.sharding import PartitionSpec as P

EDGE = 16
FIELDS = 5
SLOTS = 3
LANES = 128
BLOCK_ROWS = 2 * EDGE * FIELDS
OUTER = (0, 1, EDGE - 1, EDGE - 2)

ROW = 16
RELAY = 7

heat_ratio = 1.4
courant = 0.07

VMEM_LIMIT = 16 * 1024 * 1024


def square_moves():
    for slot in range(SLOTS):
        for field in range(FIELDS):
            for half in range(2):
                here = pl.ds((slot * FIELDS + field) * 2 * EDGE + half, EDGE, stride=2)
                there = slice(half * 64 + slot * EDGE, half * 64 + (slot + 1) * EDGE)
                yield slot, field, half, here, there


def comb(number):
    return pl.ds(number, 8, stride=EDGE)


def band(number):
    return slice(number * EDGE, (number + 1) * EDGE)


def face_planes(axis):
    return [(field, place) for field in range(FIELDS) for place in range(2 if axis == 1 else 4)]


def carried(axis, number):
    return number % 4 == 3


def face_rows(axis, number):
    size = EDGE if axis == 1 else 8
    base = (0, 15 * 8, 15 * 8 + 8 * EDGE)[axis] + (number - number // 4) * size
    return slice(base, base + size)


FACE_ROWS = 15 * 8 + 8 * EDGE + 15 * 8


def face_plane(upright, turned, axis, field, place):
    if axis == 0:
        return upright[field, comb(OUTER[place]), :]
    if axis == 2:
        return turned[field, comb(OUTER[place]), :]
    return jnp.where(lanes_of(EDGE) < 64, turned[field, band(place), :], turned[field, band(7 - place), :])


def fourth_slot(axis):
    if axis == 0:
        return (lax.broadcasted_iota(jnp.int32, (8, LANES), 0) & 3) == 3
    return ((lanes_of(EDGE if axis == 1 else 8) >> 4) & 3) == 3


def lanes_of(rows):
    return lax.broadcasted_iota(jnp.int32, (rows, LANES), 1)


def primitives(cells):
    inverse = 1.0 / cells[0]
    v1, v2, v3 = cells[1] * inverse, cells[2] * inverse, cells[3] * inverse
    square = v1 * v1 + v2 * v2 + v3 * v3
    pressure = (heat_ratio - 1.0) * (cells[4] - 0.5 * cells[0] * square)
    return cells[0], v1, v2, v3, pressure


def prepare_kernel(state, upright, turned, faces):
    for half in range(2):
        for slot in range(SLOTS):
            cells = [
                state[pl.ds((slot * FIELDS + field) * 2 * EDGE + half, EDGE, stride=2), :]
                for field in range(FIELDS)
            ]
            for field, value in enumerate(primitives(cells)):
                upright[field, band(4 * half + slot), :] = value
                if slot == SLOTS - 1:
                    upright[field, band(4 * half + slot + 1), :] = value
    for field in range(FIELDS):
        turned[field] = upright[field].T
    for axis in range(3):
        planes = face_planes(axis)
        fourth = fourth_slot(axis)
        for number, (field, place) in enumerate(planes):
            if carried(axis, number):
                continue
            value = face_plane(upright, turned, axis, field, place)
            rider = number | 3
            if rider < len(planes):
                other = face_plane(upright, turned, axis, *planes[rider])
                shift = 3 - number % 4
                other = pltpu.roll(other, shift, 0) if axis == 0 else pltpu.roll(other, shift * EDGE, 1)
                value = jnp.where(fourth, other, value)
            faces[face_rows(axis, number), :] = value


SQUARES = jax.ShapeDtypeStruct((FIELDS, LANES, LANES), jnp.float32)


def prepare(state):
    return pl.pallas_call(
        prepare_kernel,
        out_shape=(SQUARES, SQUARES, jax.ShapeDtypeStruct((FACE_ROWS, LANES), jnp.float32)),
        compiler_params=pltpu.CompilerParams(vmem_limit_bytes=VMEM_LIMIT),
        name="prepare",
    )(state)


def minmod(first, second):
    return jnp.maximum(jnp.minimum(first, second), 0.0) + jnp.minimum(
        jnp.maximum(first, second), 0.0
    )


def side_speeds(prim, component):
    scaled = heat_ratio * prim[4]
    sound = scaled * lax.rsqrt(scaled * prim[0])
    return prim[component] - sound, prim[component] + sound


def hll_flux(left, right, component):
    slow_left, fast_left = side_speeds(left, component)
    slow_right, fast_right = side_speeds(right, component)
    slow = jnp.minimum(jnp.minimum(slow_left, slow_right), 0.0)
    fast = jnp.maximum(jnp.maximum(fast_left, fast_right), 0.0)
    inverse = 1.0 / (fast - slow)
    weight_left = fast * inverse
    weight_right = -slow * inverse
    product = slow * weight_left
    normal_left, normal_right = left[component], right[component]
    carry_left = weight_left * normal_left - product
    carry_right = weight_right * normal_right + product
    mass_left, mass_right = carry_left * left[0], carry_right * right[0]
    push_left, push_right = weight_left * left[4], weight_right * right[4]
    outputs = [mass_left + mass_right]
    for number in (1, 2, 3):
        value = mass_left * left[number] + mass_right * right[number]
        if number == component:
            value = value + (push_left + push_right)
        outputs.append(value)
    square_left = left[1] * left[1] + left[2] * left[2] + left[3] * left[3]
    square_right = right[1] * right[1] + right[2] * right[2] + right[3] * right[3]
    inner = 1.0 / (heat_ratio - 1.0)
    energy = 0.5 * (mass_left * square_left + mass_right * square_right)
    energy = energy + inner * (carry_left * left[4] + carry_right * right[4])
    energy = energy + (push_left * normal_left + push_right * normal_right)
    outputs.append(energy)
    return outputs


def half_slopes(before, here, after):
    return [0.5 * minmod(b - a, c - b) for a, b, c in zip(before, here, after)]


def add(first, second):
    return [a + b for a, b in zip(first, second)]


def sub(first, second):
    return [a - b for a, b in zip(first, second)]


GROUPS = 5


def ghost_codes(links, codes):
    lane = lanes_of(EDGE)
    row = lax.broadcasted_iota(jnp.int32, (EDGE, LANES), 0)

    def by_slot(slot, face, part):
        last = links[2, part, face]
        return jnp.where(slot == 0, links[0, part, face], jnp.where(slot == 1, links[1, part, face], last))

    for side in range(2):
        slot = row & 3
        codes[side, 0] = by_slot(slot, side, 0)
        codes[side, 1] = (row & 4) + by_slot(slot, side, 1)
    slot = (lane >> 4) & 3
    inside = lane & (EDGE - 1)
    low_half = lane < 64
    for part in range(2):
        value = jnp.where(low_half, by_slot(slot, 2, part), by_slot(slot, 3, part))
        if part == 1:
            value = 64 - (lane & 64) + value * EDGE + inside
        codes[2, part] = value
    for side in range(2):
        codes[3 + side, 0] = by_slot(slot, 4 + side, 0)
        codes[3 + side, 1] = (lane & 64) + by_slot(slot, 4 + side, 1) * EDGE + inside


def inner_line(cell, size, component, store):
    before, here = cell(0), cell(1)
    left, flux = None, None
    for number in range(1, size - 1):
        after = cell(number + 1)
        slopes = half_slopes(before, here, after)
        if left is not None:
            next_flux = hll_flux(left, sub(here, slopes), component)
            store(number - 1, next_flux if flux is None else sub(next_flux, flux))
            flux = next_flux
        left = add(here, slopes)
        before, here = here, after
    store(size - 2, [-value for value in flux])


def inner_kernel(upright, turned, links, up_change, turned_change, codes):
    def store_comb(change):
        def store(number, values):
            for field in range(FIELDS):
                change[field, comb(number), :] = values[field]

        return store

    def add_band(number, values):
        for field in range(FIELDS):
            turned_change[field, band(number), :] += values[field]

    nothing = [jnp.zeros((8, LANES), jnp.float32)] * FIELDS
    for change in (up_change, turned_change):
        for number in (0, EDGE - 1):
            store_comb(change)(number, nothing)
    inner_line(
        lambda number: [upright[field, comb(number), :] for field in range(FIELDS)],
        EDGE,
        1,
        store_comb(up_change),
    )
    inner_line(
        lambda number: [turned[field, comb(number), :] for field in range(FIELDS)],
        EDGE,
        3,
        store_comb(turned_change),
    )
    inner_line(
        lambda number: [turned[field, band(number), :] for field in range(FIELDS)],
        8,
        2,
        add_band,
    )
    ghost_codes(links, codes)


def interior(upright, turned, links):
    vmem = pl.BlockSpec(memory_space=pltpu.VMEM)
    return pl.pallas_call(
        inner_kernel,
        out_shape=(
            SQUARES,
            SQUARES,
            jax.ShapeDtypeStruct((GROUPS, 2, EDGE, LANES), jnp.int32),
        ),
        in_specs=[vmem, vmem, pl.BlockSpec(memory_space=pltpu.SMEM)],
        out_specs=(vmem,) * 3,
        compiler_params=pltpu.CompilerParams(vmem_limit_bytes=VMEM_LIMIT),
        cost_estimate=pl.CostEstimate(flops=6_000_000, bytes_accessed=3_000_000, transcendentals=0),
        name="interior",
    )(upright, turned, links)


def final_counts(counts, sub_index, rounds):
    size = counts.shape[-1]
    now = [counts[0, position] for position in range(size)]

    def own(values):
        picked = values[0]
        for position in range(1, size):
            picked = jnp.where(sub_index == position, values[position], picked)
        return picked

    start = own(now)
    arrival = jnp.int32(-1)
    for bit in range(rounds):
        gains = [
            jnp.maximum(now[p ^ (1 << bit)] - now[p], 0) // 2
            - jnp.maximum(now[p] - now[p ^ (1 << bit)], 0) // 2
            for p in range(size)
        ]
        arrival = jnp.where(own(gains) > 0, bit, arrival)
        now = [value + gain for value, gain in zip(now, gains)]
    return start, own(now), arrival


def outer_side(near, far, first, second, third, side, component):
    slopes = half_slopes(near, first, second)
    if side == 0:
        beyond = add(near, half_slopes(far, near, first))
        within = sub(second, half_slopes(first, second, third))
        outside = hll_flux(beyond, sub(first, slopes), component)
        inside = hll_flux(add(first, slopes), within, component)
        return sub(inside, outside), [-value for value in inside]
    slopes = half_slopes(second, first, near)
    beyond = sub(near, half_slopes(first, near, far))
    within = add(second, half_slopes(third, second, first))
    outside = hll_flux(add(first, slopes), beyond, component)
    inside = hll_flux(within, sub(first, slopes), component)
    return sub(outside, inside), inside


def outer_kernel(
    state,
    upright,
    turned,
    up_change,
    turned_change,
    codes,
    own_faces,
    high_crossing,
    high_faces,
    low_faces,
    early_faces,
    total,
    moved,
    fixed,
):
    block = lax.axis_index("blocks")
    first_of_row = (block > 0) & (block % ROW == 0)

    def ghost(group, axis, place, mirror, field):
        rows = 8 if axis != 1 else EDGE
        owner, source = codes[group, 0, 0:rows, :], codes[group, 1, 0:rows, :]
        number = face_planes(axis).index((field, mirror))

        def fetch(stored, index):
            there = face_rows(axis, stored)
            above = high_faces[there, :] + high_crossing[there, :]
            below = jnp.where(first_of_row, early_faces[there, :], low_faces[there, :])
            low, own, high = (
                jnp.take_along_axis(values, index, axis=0 if axis == 0 else 1)
                for values in (below, own_faces[there, :], above)
            )
            return jnp.where(owner == 0, low, jnp.where(owner == 1, own, high))

        if carried(axis, number):
            slot = source & 3 if axis == 0 else (source >> 4) & 3
            index = source | (3 if axis == 0 else 3 * EDGE)
            first, second, third = (fetch(number - 3 + carrier, index) for carrier in range(3))
            neighbour = jnp.where(slot == 0, first, jnp.where(slot == 1, second, third))
        else:
            neighbour = fetch(number, source)
        return jnp.where(owner == 3, face_plane(upright, turned, axis, field, place), neighbour)

    low_half = lanes_of(EDGE) < 64
    for field in range(FIELDS):
        fixed[field] = turned_change[field]

    cells = {
        number: [turned[field, band(number), :] for field in range(FIELDS)]
        for number in (0, 1, 2, 5, 6, 7)
    }
    ghosts = [[ghost(2, 1, depth, depth, field) for field in range(FIELDS)] for depth in range(2)]
    for side in range(2):
        numbers = (0, 1, 2) if side == 0 else (7, 6, 5)
        outside = []
        for depth in range(2):
            other = cells[7 - depth if side == 0 else depth]
            across = [pltpu.roll(value, 64, 1) for value in other]
            pair = (ghosts[depth], across) if side == 0 else (across, ghosts[depth])
            outside.append([jnp.where(low_half, a, b) for a, b in zip(*pair)])
        parts = outer_side(*outside, *(cells[number] for number in numbers), side, 2)
        for number, part in zip(numbers, parts):
            for field in range(FIELDS):
                fixed[field, band(number), :] += part[field]

    def comb_sides(square, axis, group, change):
        for side in range(2):
            numbers = (0, 1, 2) if side == 0 else (EDGE - 1, EDGE - 2, EDGE - 3)
            planes = [
                [square[field, comb(number), :] for field in range(FIELDS)] for number in numbers
            ]
            outside = [
                [
                    ghost(group + side, axis, 2 * side + depth, 2 * (1 - side) + depth, field)
                    for field in range(FIELDS)
                ]
                for depth in range(2)
            ]
            parts = outer_side(*outside, *planes, side, axis + 1)
            for number, part in zip(numbers, parts):
                for field in range(FIELDS):
                    change[field, comb(number), :] += part[field]

    comb_sides(turned, 2, 3, fixed)
    for field in range(FIELDS):
        total[field] = up_change[field] + fixed[field].T
    comb_sides(upright, 0, 0, total)

    for slot, field, half, here, there in square_moves():
        if slot == SLOTS - 1:
            moved[pl.ds(field * 2 * EDGE + half, EDGE, stride=2), :] = (
                state[here, :] - courant * total[field, there, :]
            )


def outer(*operands):
    vmem = pl.BlockSpec(memory_space=pltpu.VMEM)
    return pl.pallas_call(
        outer_kernel,
        out_shape=(SQUARES, jax.ShapeDtypeStruct((BLOCK_ROWS, LANES), jnp.float32)),
        in_specs=[vmem] * len(operands),
        out_specs=(vmem, vmem),
        scratch_shapes=[pltpu.VMEM(SQUARES.shape, jnp.float32)],
        compiler_params=pltpu.CompilerParams(vmem_limit_bytes=VMEM_LIMIT),
        name="outer",
    )(*operands)


def finish_kernel(rounds, state, total, counts, out, second, arrival):
    _, last_count, arrival_round = final_counts(counts, lax.axis_index("sub"), rounds)
    arrival[...] = jnp.full(arrival.shape, arrival_round, jnp.int32)
    for slot, field, half, here, there in square_moves():
        fresh = state[here, :] - courant * total[field, there, :]
        fresh = jnp.where(slot < last_count, fresh, 0.0)
        out[here, :] = fresh
        if slot == 1:
            second[pl.ds(field * 2 * EDGE + half, EDGE, stride=2), :] = fresh


def finish(state, total, counts, rounds):
    vmem = pl.BlockSpec(memory_space=pltpu.VMEM)
    smem = pl.BlockSpec(memory_space=pltpu.SMEM)
    return pl.pallas_call(
        functools.partial(finish_kernel, rounds),
        out_shape=(
            jax.ShapeDtypeStruct(state.shape, jnp.float32),
            jax.ShapeDtypeStruct((BLOCK_ROWS, LANES), jnp.float32),
            jax.ShapeDtypeStruct((8, LANES), jnp.int32),
        ),
        in_specs=[vmem, vmem, smem],
        out_specs=(vmem,) * 3,
        compiler_params=pltpu.CompilerParams(vmem_limit_bytes=VMEM_LIMIT),
        cost_estimate=pl.CostEstimate(flops=200_000, bytes_accessed=1_000_000, transcendentals=0),
        name="finish",
    )(state, total, counts)


def place_kernel(rounds, *refs):
    arrived, (second, arrival, _, out, block, sem) = refs[:rounds], refs[rounds:]
    arrival_round = arrival[...]
    for row in range(0, BLOCK_ROWS, 8):
        rows = slice(row, row + 8)
        value = second[rows, :]
        for bit in range(rounds):
            value = jnp.where(arrival_round == bit, arrived[bit][rows, :], value)
        block[rows, :] = value
    copy = pltpu.make_async_copy(block, out.at[pl.ds(BLOCK_ROWS, BLOCK_ROWS)], sem)
    copy.start()
    copy.wait()


def place(arrived, out, second, arrival):
    rounds = len(arrived)
    vmem = pl.BlockSpec(memory_space=pltpu.VMEM)
    anywhere = pl.BlockSpec(memory_space=pl.ANY)
    return pl.pallas_call(
        functools.partial(place_kernel, rounds),
        out_shape=jax.ShapeDtypeStruct(out.shape, out.dtype),
        in_specs=[vmem] * (rounds + 2) + [anywhere],
        out_specs=anywhere,
        scratch_shapes=[
            pltpu.VMEM((BLOCK_ROWS, LANES), jnp.float32),
            pltpu.SemaphoreType.DMA,
        ],
        input_output_aliases={rounds + 2: 0},
        compiler_params=pltpu.CompilerParams(vmem_limit_bytes=1024 * 1024),
        name="place",
    )(*arrived, second, arrival, out)


def body(state, neighbours, counts):
    size = lax.axis_size("blocks")
    rounds = lax.axis_size("sub").bit_length() - 1
    shape = state.shape
    state = state.reshape(SLOTS * BLOCK_ROWS, LANES)
    links = jnp.transpose(neighbours.reshape(SLOTS, 6, 2), (0, 2, 1))
    upright, turned, faces = prepare(state)
    firsts = range(ROW, size, ROW)
    forward = [(i, i + 1) for i in range(size - 1) if i + 1 not in firsts]
    backward = [(i + 1, i) for i in range(size - 1) if i + 1 not in firsts]
    low = lax.ppermute(faces, "blocks", forward)
    high = lax.ppermute(faces, "blocks", backward)
    changes = interior(upright, turned, links)
    early = [(i, i - ROW + RELAY) for i in firsts] + [(i - 1, i) for i in firsts]
    relayed = lax.ppermute(faces, "blocks", early)
    held, *changes = lax.optimization_barrier((relayed, *changes))
    crossing = lax.ppermute(held, "blocks", [(i - ROW + RELAY, i - 1) for i in firsts])
    total, moved = outer(state, upright, turned, *changes, faces, crossing, high, low, relayed)
    arrived = [
        lax.ppermute(
            moved, "sub", [(s, s ^ (1 << bit)) for s in range(lax.axis_size("sub"))]
        )
        for bit in range(rounds)
    ]
    out, second, arrival = finish(state, total, counts, rounds)
    return place(arrived, out, second, arrival).reshape(shape)


def solution(mesh):
    return jax.shard_map(
        body,
        mesh=mesh,
        in_specs=(
            P("blocks", "sub", None, None, None),
            P("blocks", "sub", None, None, None),
            P("blocks", None),
        ),
        out_specs=P("blocks", "sub", None, None, None),
        check_vma=False,
    )
```

```python
import functools

import jax
import jax.numpy as jnp
from jax import lax
from jax.experimental import pallas as pl
from jax.experimental.pallas import tpu as pltpu
from jax.sharding import PartitionSpec as P

EDGE = 16
FIELDS = 5
SLOTS = 3
LANES = 128
BLOCK_ROWS = 2 * EDGE * FIELDS
OUTER = (0, 1, EDGE - 1, EDGE - 2)

SEND_ORDER = (0, 2, 1)
ROW = 16
RELAY = 7

heat_ratio = 1.4
courant = 0.07

VMEM_LIMIT = 16 * 1024 * 1024


def square_moves():
    for slot in range(SLOTS):
        for field in range(FIELDS):
            for half in range(2):
                here = pl.ds((slot * FIELDS + field) * 2 * EDGE + half, EDGE, stride=2)
                there = slice(half * 64 + slot * EDGE, half * 64 + (slot + 1) * EDGE)
                yield slot, field, half, here, there


def comb(number):
    return pl.ds(number, 8, stride=EDGE)


def band(number):
    return slice(number * EDGE, (number + 1) * EDGE)


def face_planes(axis):
    return [(field, place) for field in range(FIELDS) for place in range(2 if axis == 1 else 4)]


def carried(axis, number):
    return number % 4 == 3


def face_rows(axis, number):
    size = EDGE if axis == 1 else 8
    base = (0, 15 * 8, 15 * 8 + 8 * EDGE)[axis] + (number - number // 4) * size
    return slice(base, base + size)


FACE_ROWS = 15 * 8 + 8 * EDGE + 15 * 8


def face_plane(upright, turned, axis, field, place):
    if axis == 0:
        return upright[field, comb(OUTER[place]), :]
    if axis == 2:
        return turned[field, comb(OUTER[place]), :]
    return jnp.where(lanes_of(EDGE) < 64, turned[field, band(place), :], turned[field, band(7 - place), :])


def fourth_slot(axis):
    if axis == 0:
        return (lax.broadcasted_iota(jnp.int32, (8, LANES), 0) & 3) == 3
    return ((lanes_of(EDGE if axis == 1 else 8) >> 4) & 3) == 3


def lanes_of(rows):
    return lax.broadcasted_iota(jnp.int32, (rows, LANES), 1)


def primitives(cells):
    inverse = 1.0 / cells[0]
    v1, v2, v3 = cells[1] * inverse, cells[2] * inverse, cells[3] * inverse
    square = v1 * v1 + v2 * v2 + v3 * v3
    pressure = (heat_ratio - 1.0) * (cells[4] - 0.5 * cells[0] * square)
    return cells[0], v1, v2, v3, pressure


def prepare_kernel(state, upright, turned, faces):
    for half in range(2):
        for slot in range(SLOTS):
            cells = [
                state[pl.ds((slot * FIELDS + field) * 2 * EDGE + half, EDGE, stride=2), :]
                for field in range(FIELDS)
            ]
            for field, value in enumerate(primitives(cells)):
                upright[field, band(4 * half + slot), :] = value
                if slot == SLOTS - 1:
                    upright[field, band(4 * half + slot + 1), :] = value
    for field in range(FIELDS):
        turned[field] = upright[field].T
    for axis in range(3):
        planes = face_planes(axis)
        fourth = fourth_slot(axis)
        for number, (field, place) in enumerate(planes):
            if carried(axis, number):
                continue
            value = face_plane(upright, turned, axis, field, place)
            rider = number | 3
            if rider < len(planes):
                other = face_plane(upright, turned, axis, *planes[rider])
                shift = 3 - number % 4
                other = pltpu.roll(other, shift, 0) if axis == 0 else pltpu.roll(other, shift * EDGE, 1)
                value = jnp.where(fourth, other, value)
            faces[face_rows(axis, number), :] = value


SQUARES = jax.ShapeDtypeStruct((FIELDS, LANES, LANES), jnp.float32)


def prepare(state):
    return pl.pallas_call(
        prepare_kernel,
        out_shape=(SQUARES, SQUARES, jax.ShapeDtypeStruct((FACE_ROWS, LANES), jnp.float32)),
        compiler_params=pltpu.CompilerParams(vmem_limit_bytes=VMEM_LIMIT),
        name="prepare",
    )(state)


def minmod(first, second):
    return jnp.maximum(jnp.minimum(first, second), 0.0) + jnp.minimum(
        jnp.maximum(first, second), 0.0
    )


def side_speeds(prim, component):
    scaled = heat_ratio * prim[4]
    sound = scaled * lax.rsqrt(scaled * prim[0])
    return prim[component] - sound, prim[component] + sound


def hll_flux(left, right, component):
    slow_left, fast_left = side_speeds(left, component)
    slow_right, fast_right = side_speeds(right, component)
    slow = jnp.minimum(jnp.minimum(slow_left, slow_right), 0.0)
    fast = jnp.maximum(jnp.maximum(fast_left, fast_right), 0.0)
    inverse = 1.0 / (fast - slow)
    weight_left = fast * inverse
    weight_right = -slow * inverse
    product = slow * weight_left
    normal_left, normal_right = left[component], right[component]
    carry_left = weight_left * normal_left - product
    carry_right = weight_right * normal_right + product
    mass_left, mass_right = carry_left * left[0], carry_right * right[0]
    push_left, push_right = weight_left * left[4], weight_right * right[4]
    outputs = [mass_left + mass_right]
    for number in (1, 2, 3):
        value = mass_left * left[number] + mass_right * right[number]
        if number == component:
            value = value + (push_left + push_right)
        outputs.append(value)
    square_left = left[1] * left[1] + left[2] * left[2] + left[3] * left[3]
    square_right = right[1] * right[1] + right[2] * right[2] + right[3] * right[3]
    inner = 1.0 / (heat_ratio - 1.0)
    energy = 0.5 * (mass_left * square_left + mass_right * square_right)
    energy = energy + inner * (carry_left * left[4] + carry_right * right[4])
    energy = energy + (push_left * normal_left + push_right * normal_right)
    outputs.append(energy)
    return outputs


def half_slopes(before, here, after):
    return [0.5 * minmod(b - a, c - b) for a, b, c in zip(before, here, after)]


def add(first, second):
    return [a + b for a, b in zip(first, second)]


def sub(first, second):
    return [a - b for a, b in zip(first, second)]


GROUPS = 5


def ghost_codes(links, codes):
    lane = lanes_of(EDGE)
    row = lax.broadcasted_iota(jnp.int32, (EDGE, LANES), 0)

    def by_slot(slot, face, part):
        last = links[2, part, face]
        return jnp.where(slot == 0, links[0, part, face], jnp.where(slot == 1, links[1, part, face], last))

    for side in range(2):
        slot = row & 3
        codes[side, 0] = by_slot(slot, side, 0)
        codes[side, 1] = (row & 4) + by_slot(slot, side, 1)
    slot = (lane >> 4) & 3
    inside = lane & (EDGE - 1)
    low_half = lane < 64
    for part in range(2):
        value = jnp.where(low_half, by_slot(slot, 2, part), by_slot(slot, 3, part))
        if part == 1:
            value = 64 - (lane & 64) + value * EDGE + inside
        codes[2, part] = value
    for side in range(2):
        codes[3 + side, 0] = by_slot(slot, 4 + side, 0)
        codes[3 + side, 1] = (lane & 64) + by_slot(slot, 4 + side, 1) * EDGE + inside


def inner_line(cell, size, component, store):
    before, here = cell(0), cell(1)
    left, flux = None, None
    for number in range(1, size - 1):
        after = cell(number + 1)
        slopes = half_slopes(before, here, after)
        if left is not None:
            next_flux = hll_flux(left, sub(here, slopes), component)
            store(number - 1, next_flux if flux is None else sub(next_flux, flux))
            flux = next_flux
        left = add(here, slopes)
        before, here = here, after
    store(size - 2, [-value for value in flux])


def inner_kernel(upright, turned, links, up_change, turned_change, codes):
    def store_comb(change):
        def store(number, values):
            for field in range(FIELDS):
                change[field, comb(number), :] = values[field]

        return store

    def add_band(number, values):
        for field in range(FIELDS):
            turned_change[field, band(number), :] += values[field]

    nothing = [jnp.zeros((8, LANES), jnp.float32)] * FIELDS
    for change in (up_change, turned_change):
        for number in (0, EDGE - 1):
            store_comb(change)(number, nothing)
    inner_line(
        lambda number: [upright[field, comb(number), :] for field in range(FIELDS)],
        EDGE,
        1,
        store_comb(up_change),
    )
    inner_line(
        lambda number: [turned[field, comb(number), :] for field in range(FIELDS)],
        EDGE,
        3,
        store_comb(turned_change),
    )
    inner_line(
        lambda number: [turned[field, band(number), :] for field in range(FIELDS)],
        8,
        2,
        add_band,
    )
    ghost_codes(links, codes)


def interior(upright, turned, links):
    vmem = pl.BlockSpec(memory_space=pltpu.VMEM)
    return pl.pallas_call(
        inner_kernel,
        out_shape=(
            SQUARES,
            SQUARES,
            jax.ShapeDtypeStruct((GROUPS, 2, EDGE, LANES), jnp.int32),
        ),
        in_specs=[vmem, vmem, pl.BlockSpec(memory_space=pltpu.SMEM)],
        out_specs=(vmem,) * 3,
        compiler_params=pltpu.CompilerParams(vmem_limit_bytes=VMEM_LIMIT),
        cost_estimate=pl.CostEstimate(flops=6_000_000, bytes_accessed=3_000_000, transcendentals=0),
        name="interior",
    )(upright, turned, links)


def final_counts(counts, sub_index, rounds):
    size = counts.shape[-1]
    now = [counts[0, position] for position in range(size)]

    def own(values):
        picked = values[0]
        for position in range(1, size):
            picked = jnp.where(sub_index == position, values[position], picked)
        return picked

    start = own(now)
    arrival = jnp.int32(-1)
    for bit in range(rounds):
        gains = [
            jnp.maximum(now[p ^ (1 << bit)] - now[p], 0) // 2
            - jnp.maximum(now[p] - now[p ^ (1 << bit)], 0) // 2
            for p in range(size)
        ]
        arrival = jnp.where(own(gains) > 0, bit, arrival)
        now = [value + gain for value, gain in zip(now, gains)]
    return start, own(now), arrival


def outer_side(near, far, first, second, third, side, component):
    slopes = half_slopes(near, first, second)
    if side == 0:
        beyond = add(near, half_slopes(far, near, first))
        within = sub(second, half_slopes(first, second, third))
        outside = hll_flux(beyond, sub(first, slopes), component)
        inside = hll_flux(add(first, slopes), within, component)
        return sub(inside, outside), [-value for value in inside]
    slopes = half_slopes(second, first, near)
    beyond = sub(near, half_slopes(first, near, far))
    within = add(second, half_slopes(third, second, first))
    outside = hll_flux(add(first, slopes), beyond, component)
    inside = hll_flux(within, sub(first, slopes), component)
    return sub(outside, inside), inside


def outer_kernel(
    state,
    upright,
    turned,
    up_change,
    turned_change,
    codes,
    own_faces,
    high_crossing,
    high_faces,
    low_faces,
    early_faces,
    total,
    moved,
    fixed,
):
    block = lax.axis_index("blocks")
    first_of_row = (block > 0) & (block % ROW == 0)

    def ghost(group, axis, place, mirror, field):
        rows = 8 if axis != 1 else EDGE
        owner, source = codes[group, 0, 0:rows, :], codes[group, 1, 0:rows, :]
        number = face_planes(axis).index((field, mirror))

        def fetch(stored, index):
            there = face_rows(axis, stored)
            above = high_faces[there, :] + high_crossing[there, :]
            below = jnp.where(first_of_row, early_faces[there, :], low_faces[there, :])
            low, own, high = (
                jnp.take_along_axis(values, index, axis=0 if axis == 0 else 1)
                for values in (below, own_faces[there, :], above)
            )
            return jnp.where(owner == 0, low, jnp.where(owner == 1, own, high))

        if carried(axis, number):
            slot = source & 3 if axis == 0 else (source >> 4) & 3
            index = source | (3 if axis == 0 else 3 * EDGE)
            first, second, third = (fetch(number - 3 + carrier, index) for carrier in range(3))
            neighbour = jnp.where(slot == 0, first, jnp.where(slot == 1, second, third))
        else:
            neighbour = fetch(number, source)
        return jnp.where(owner == 3, face_plane(upright, turned, axis, field, place), neighbour)

    low_half = lanes_of(EDGE) < 64
    for field in range(FIELDS):
        fixed[field] = turned_change[field]

    cells = {
        number: [turned[field, band(number), :] for field in range(FIELDS)]
        for number in (0, 1, 2, 5, 6, 7)
    }
    ghosts = [[ghost(2, 1, depth, depth, field) for field in range(FIELDS)] for depth in range(2)]
    for side in range(2):
        numbers = (0, 1, 2) if side == 0 else (7, 6, 5)
        outside = []
        for depth in range(2):
            other = cells[7 - depth if side == 0 else depth]
            across = [pltpu.roll(value, 64, 1) for value in other]
            pair = (ghosts[depth], across) if side == 0 else (across, ghosts[depth])
            outside.append([jnp.where(low_half, a, b) for a, b in zip(*pair)])
        parts = outer_side(*outside, *(cells[number] for number in numbers), side, 2)
        for number, part in zip(numbers, parts):
            for field in range(FIELDS):
                fixed[field, band(number), :] += part[field]

    def comb_sides(square, axis, group, change):
        for side in range(2):
            numbers = (0, 1, 2) if side == 0 else (EDGE - 1, EDGE - 2, EDGE - 3)
            planes = [
                [square[field, comb(number), :] for field in range(FIELDS)] for number in numbers
            ]
            outside = [
                [
                    ghost(group + side, axis, 2 * side + depth, 2 * (1 - side) + depth, field)
                    for field in range(FIELDS)
                ]
                for depth in range(2)
            ]
            parts = outer_side(*outside, *planes, side, axis + 1)
            for number, part in zip(numbers, parts):
                for field in range(FIELDS):
                    change[field, comb(number), :] += part[field]

    comb_sides(turned, 2, 3, fixed)
    for field in range(FIELDS):
        total[field] = up_change[field] + fixed[field].T
    comb_sides(upright, 0, 0, total)

    for slot, field, half, here, there in square_moves():
        if slot == SLOTS - 1:
            moved[pl.ds(field * 2 * EDGE + half, EDGE, stride=2), :] = (
                state[here, :] - courant * total[field, there, :]
            )


def outer(*operands):
    vmem = pl.BlockSpec(memory_space=pltpu.VMEM)
    return pl.pallas_call(
        outer_kernel,
        out_shape=(SQUARES, jax.ShapeDtypeStruct((BLOCK_ROWS, LANES), jnp.float32)),
        in_specs=[vmem] * len(operands),
        out_specs=(vmem, vmem),
        scratch_shapes=[pltpu.VMEM(SQUARES.shape, jnp.float32)],
        compiler_params=pltpu.CompilerParams(vmem_limit_bytes=VMEM_LIMIT),
        name="outer",
    )(*operands)


def finish_kernel(rounds, state, total, counts, out, second, arrival):
    _, last_count, arrival_round = final_counts(counts, lax.axis_index("sub"), rounds)
    arrival[...] = jnp.full(arrival.shape, arrival_round, jnp.int32)
    for slot, field, half, here, there in square_moves():
        fresh = state[here, :] - courant * total[field, there, :]
        fresh = jnp.where(slot < last_count, fresh, 0.0)
        out[here, :] = fresh
        if slot == 1:
            second[pl.ds(field * 2 * EDGE + half, EDGE, stride=2), :] = fresh


def finish(state, total, counts, rounds):
    vmem = pl.BlockSpec(memory_space=pltpu.VMEM)
    smem = pl.BlockSpec(memory_space=pltpu.SMEM)
    return pl.pallas_call(
        functools.partial(finish_kernel, rounds),
        out_shape=(
            jax.ShapeDtypeStruct(state.shape, jnp.float32),
            jax.ShapeDtypeStruct((BLOCK_ROWS, LANES), jnp.float32),
            jax.ShapeDtypeStruct((8, LANES), jnp.int32),
        ),
        in_specs=[vmem, vmem, smem],
        out_specs=(vmem,) * 3,
        compiler_params=pltpu.CompilerParams(vmem_limit_bytes=VMEM_LIMIT),
        cost_estimate=pl.CostEstimate(flops=200_000, bytes_accessed=1_000_000, transcendentals=0),
        name="finish",
    )(state, total, counts)


def place_kernel(rounds, *refs):
    arrived, (second, arrival, _, out, block, sem) = refs[:rounds], refs[rounds:]
    arrived = dict(zip(SEND_ORDER, arrived))
    arrival_round = arrival[...]
    for row in range(0, BLOCK_ROWS, 8):
        rows = slice(row, row + 8)
        value = second[rows, :]
        for bit in range(rounds):
            value = jnp.where(arrival_round == bit, arrived[bit][rows, :], value)
        block[rows, :] = value
    copy = pltpu.make_async_copy(block, out.at[pl.ds(BLOCK_ROWS, BLOCK_ROWS)], sem)
    copy.start()
    copy.wait()


def place(arrived, out, second, arrival):
    rounds = len(arrived)
    vmem = pl.BlockSpec(memory_space=pltpu.VMEM)
    anywhere = pl.BlockSpec(memory_space=pl.ANY)
    return pl.pallas_call(
        functools.partial(place_kernel, rounds),
        out_shape=jax.ShapeDtypeStruct(out.shape, out.dtype),
        in_specs=[vmem] * (rounds + 2) + [anywhere],
        out_specs=anywhere,
        scratch_shapes=[
            pltpu.VMEM((BLOCK_ROWS, LANES), jnp.float32),
            pltpu.SemaphoreType.DMA,
        ],
        input_output_aliases={rounds + 2: 0},
        compiler_params=pltpu.CompilerParams(vmem_limit_bytes=1024 * 1024),
        name="place",
    )(*arrived.values(), second, arrival, out)


def body(state, neighbours, counts):
    size = lax.axis_size("blocks")
    rounds = lax.axis_size("sub").bit_length() - 1
    shape = state.shape
    state = state.reshape(SLOTS * BLOCK_ROWS, LANES)
    links = jnp.transpose(neighbours.reshape(SLOTS, 6, 2), (0, 2, 1))
    upright, turned, faces = prepare(state)
    firsts = range(ROW, size, ROW)
    forward = [(i, i + 1) for i in range(size - 1) if i + 1 not in firsts]
    backward = [(i + 1, i) for i in range(size - 1) if i + 1 not in firsts]
    low = lax.ppermute(faces, "blocks", forward)
    high = lax.ppermute(faces, "blocks", backward)
    changes = interior(upright, turned, links)
    early = [(i, i - ROW + RELAY) for i in firsts] + [(i - 1, i) for i in firsts]
    relayed = lax.ppermute(faces, "blocks", early)
    held, *changes = lax.optimization_barrier((relayed, *changes))
    crossing = lax.ppermute(held, "blocks", [(i - ROW + RELAY, i - 1) for i in firsts])
    total, moved = outer(state, upright, turned, *changes, faces, crossing, high, low, relayed)
    arrived = {
        bit: lax.ppermute(
            moved, "sub", [(s, s ^ (1 << bit)) for s in range(lax.axis_size("sub"))]
        )
        for bit in SEND_ORDER
    }
    out, second, arrival = finish(state, total, counts, rounds)
    return place(arrived, out, second, arrival).reshape(shape)


def solution(mesh):
    return jax.shard_map(
        body,
        mesh=mesh,
        in_specs=(
            P("blocks", "sub", None, None, None),
            P("blocks", "sub", None, None, None),
            P("blocks", None),
        ),
        out_specs=P("blocks", "sub", None, None, None),
        check_vma=False,
    )
```

```python
import functools

import jax
import jax.numpy as jnp
from jax import lax
from jax.experimental import pallas as pl
from jax.experimental.pallas import tpu as pltpu
from jax.sharding import PartitionSpec as P

EDGE = 16
FIELDS = 5
SLOTS = 3
LANES = 128
BLOCK_ROWS = 2 * EDGE * FIELDS
OUTER = (0, 1, EDGE - 1, EDGE - 2)

SEND_ORDER = (0, 2, 1)
ROW = 16
RELAY = 7

heat_ratio = 1.4
courant = 0.07

VMEM_LIMIT = 16 * 1024 * 1024


def square_moves():
    for slot in range(SLOTS):
        for field in range(FIELDS):
            for half in range(2):
                here = pl.ds((slot * FIELDS + field) * 2 * EDGE + half, EDGE, stride=2)
                there = slice(half * 64 + slot * EDGE, half * 64 + (slot + 1) * EDGE)
                yield slot, field, half, here, there


def comb(number):
    return pl.ds(number, 8, stride=EDGE)


def band(number):
    return slice(number * EDGE, (number + 1) * EDGE)


def face_planes(axis):
    return [(field, place) for field in range(FIELDS) for place in range(2 if axis == 1 else 4)]


def carried(axis, number):
    return number % 4 == 3


def face_rows(axis, number):
    size = EDGE if axis == 1 else 8
    base = (0, 15 * 8, 15 * 8 + 8 * EDGE)[axis] + (number - number // 4) * size
    return slice(base, base + size)


FACE_ROWS = 15 * 8 + 8 * EDGE + 15 * 8


def face_plane(upright, turned, axis, field, place):
    if axis == 0:
        return upright[field, comb(OUTER[place]), :]
    if axis == 2:
        return turned[field, comb(OUTER[place]), :]
    return jnp.where(lanes_of(EDGE) < 64, turned[field, band(place), :], turned[field, band(7 - place), :])


def fourth_slot(axis):
    if axis == 0:
        return (lax.broadcasted_iota(jnp.int32, (8, LANES), 0) & 3) == 3
    return ((lanes_of(EDGE if axis == 1 else 8) >> 4) & 3) == 3


def lanes_of(rows):
    return lax.broadcasted_iota(jnp.int32, (rows, LANES), 1)


def primitives(cells):
    inverse = 1.0 / cells[0]
    v1, v2, v3 = cells[1] * inverse, cells[2] * inverse, cells[3] * inverse
    square = v1 * v1 + v2 * v2 + v3 * v3
    pressure = (heat_ratio - 1.0) * (cells[4] - 0.5 * cells[0] * square)
    return cells[0], v1, v2, v3, pressure


def prepare_kernel(state, upright, turned, faces):
    for half in range(2):
        for slot in range(SLOTS):
            cells = [
                state[pl.ds((slot * FIELDS + field) * 2 * EDGE + half, EDGE, stride=2), :]
                for field in range(FIELDS)
            ]
            for field, value in enumerate(primitives(cells)):
                upright[field, band(4 * half + slot), :] = value
                if slot == SLOTS - 1:
                    upright[field, band(4 * half + slot + 1), :] = value
    for field in range(FIELDS):
        turned[field] = upright[field].T
    for axis in range(3):
        planes = face_planes(axis)
        fourth = fourth_slot(axis)
        for number, (field, place) in enumerate(planes):
            if carried(axis, number):
                continue
            value = face_plane(upright, turned, axis, field, place)
            rider = number | 3
            if rider < len(planes):
                other = face_plane(upright, turned, axis, *planes[rider])
                shift = 3 - number % 4
                other = pltpu.roll(other, shift, 0) if axis == 0 else pltpu.roll(other, shift * EDGE, 1)
                value = jnp.where(fourth, other, value)
            faces[face_rows(axis, number), :] = value


SQUARES = jax.ShapeDtypeStruct((FIELDS, LANES, LANES), jnp.float32)


def prepare(state):
    return pl.pallas_call(
        prepare_kernel,
        out_shape=(SQUARES, SQUARES, jax.ShapeDtypeStruct((FACE_ROWS, LANES), jnp.float32)),
        compiler_params=pltpu.CompilerParams(vmem_limit_bytes=VMEM_LIMIT),
        name="prepare",
    )(state)


def minmod(first, second):
    return jnp.maximum(jnp.minimum(first, second), 0.0) + jnp.minimum(
        jnp.maximum(first, second), 0.0
    )


def side_speeds(prim, component):
    scaled = heat_ratio * prim[4]
    sound = scaled * lax.rsqrt(scaled * prim[0])
    return prim[component] - sound, prim[component] + sound


def hll_flux(left, right, component):
    slow_left, fast_left = side_speeds(left, component)
    slow_right, fast_right = side_speeds(right, component)
    slow = jnp.minimum(jnp.minimum(slow_left, slow_right), 0.0)
    fast = jnp.maximum(jnp.maximum(fast_left, fast_right), 0.0)
    inverse = 1.0 / (fast - slow)
    weight_left = fast * inverse
    weight_right = -slow * inverse
    product = slow * weight_left
    normal_left, normal_right = left[component], right[component]
    carry_left = weight_left * normal_left - product
    carry_right = weight_right * normal_right + product
    mass_left, mass_right = carry_left * left[0], carry_right * right[0]
    push_left, push_right = weight_left * left[4], weight_right * right[4]
    outputs = [mass_left + mass_right]
    for number in (1, 2, 3):
        value = mass_left * left[number] + mass_right * right[number]
        if number == component:
            value = value + (push_left + push_right)
        outputs.append(value)
    square_left = left[1] * left[1] + left[2] * left[2] + left[3] * left[3]
    square_right = right[1] * right[1] + right[2] * right[2] + right[3] * right[3]
    inner = 1.0 / (heat_ratio - 1.0)
    energy = 0.5 * (mass_left * square_left + mass_right * square_right)
    energy = energy + inner * (carry_left * left[4] + carry_right * right[4])
    energy = energy + (push_left * normal_left + push_right * normal_right)
    outputs.append(energy)
    return outputs


def half_slopes(before, here, after):
    return [0.5 * minmod(b - a, c - b) for a, b, c in zip(before, here, after)]


def add(first, second):
    return [a + b for a, b in zip(first, second)]


def sub(first, second):
    return [a - b for a, b in zip(first, second)]


GROUPS = 5


def ghost_codes(links, codes):
    lane = lanes_of(EDGE)
    row = lax.broadcasted_iota(jnp.int32, (EDGE, LANES), 0)

    def by_slot(slot, face, part):
        last = links[2, part, face]
        return jnp.where(slot == 0, links[0, part, face], jnp.where(slot == 1, links[1, part, face], last))

    for side in range(2):
        slot = row & 3
        codes[side, 0] = by_slot(slot, side, 0)
        codes[side, 1] = (row & 4) + by_slot(slot, side, 1)
    slot = (lane >> 4) & 3
    inside = lane & (EDGE - 1)
    low_half = lane < 64
    for part in range(2):
        value = jnp.where(low_half, by_slot(slot, 2, part), by_slot(slot, 3, part))
        if part == 1:
            value = 64 - (lane & 64) + value * EDGE + inside
        codes[2, part] = value
    for side in range(2):
        codes[3 + side, 0] = by_slot(slot, 4 + side, 0)
        codes[3 + side, 1] = (lane & 64) + by_slot(slot, 4 + side, 1) * EDGE + inside


def inner_line(cell, size, component, store):
    before, here = cell(0), cell(1)
    left, flux = None, None
    for number in range(1, size - 1):
        after = cell(number + 1)
        slopes = half_slopes(before, here, after)
        if left is not None:
            next_flux = hll_flux(left, sub(here, slopes), component)
            store(number - 1, next_flux if flux is None else sub(next_flux, flux))
            flux = next_flux
        left = add(here, slopes)
        before, here = here, after
    store(size - 2, [-value for value in flux])


def inner_kernel(upright, turned, links, up_change, turned_change, codes):
    def store_comb(change):
        def store(number, values):
            for field in range(FIELDS):
                change[field, comb(number), :] = values[field]

        return store

    def add_band(number, values):
        for field in range(FIELDS):
            turned_change[field, band(number), :] += values[field]

    nothing = [jnp.zeros((8, LANES), jnp.float32)] * FIELDS
    for change in (up_change, turned_change):
        for number in (0, EDGE - 1):
            store_comb(change)(number, nothing)
    inner_line(
        lambda number: [upright[field, comb(number), :] for field in range(FIELDS)],
        EDGE,
        1,
        store_comb(up_change),
    )
    inner_line(
        lambda number: [turned[field, comb(number), :] for field in range(FIELDS)],
        EDGE,
        3,
        store_comb(turned_change),
    )
    inner_line(
        lambda number: [turned[field, band(number), :] for field in range(FIELDS)],
        8,
        2,
        add_band,
    )
    ghost_codes(links, codes)


def interior(upright, turned, links):
    vmem = pl.BlockSpec(memory_space=pltpu.VMEM)
    return pl.pallas_call(
        inner_kernel,
        out_shape=(
            SQUARES,
            SQUARES,
            jax.ShapeDtypeStruct((GROUPS, 2, EDGE, LANES), jnp.int32),
        ),
        in_specs=[vmem, vmem, pl.BlockSpec(memory_space=pltpu.SMEM)],
        out_specs=(vmem,) * 3,
        compiler_params=pltpu.CompilerParams(vmem_limit_bytes=VMEM_LIMIT),
        cost_estimate=pl.CostEstimate(flops=6_000_000, bytes_accessed=3_000_000, transcendentals=0),
        name="interior",
    )(upright, turned, links)


def final_counts(counts, sub_index, rounds):
    size = counts.shape[-1]
    now = [counts[0, position] for position in range(size)]

    def own(values):
        picked = values[0]
        for position in range(1, size):
            picked = jnp.where(sub_index == position, values[position], picked)
        return picked

    start = own(now)
    arrival = jnp.int32(-1)
    for bit in range(rounds):
        gains = [
            jnp.maximum(now[p ^ (1 << bit)] - now[p], 0) // 2
            - jnp.maximum(now[p] - now[p ^ (1 << bit)], 0) // 2
            for p in range(size)
        ]
        arrival = jnp.where(own(gains) > 0, bit, arrival)
        now = [value + gain for value, gain in zip(now, gains)]
    return start, own(now), arrival


def outer_side(near, far, first, second, third, side, component):
    slopes = half_slopes(near, first, second)
    if side == 0:
        beyond = add(near, half_slopes(far, near, first))
        within = sub(second, half_slopes(first, second, third))
        outside = hll_flux(beyond, sub(first, slopes), component)
        inside = hll_flux(add(first, slopes), within, component)
        return sub(inside, outside), [-value for value in inside]
    slopes = half_slopes(second, first, near)
    beyond = sub(near, half_slopes(first, near, far))
    within = add(second, half_slopes(third, second, first))
    outside = hll_flux(add(first, slopes), beyond, component)
    inside = hll_flux(within, sub(first, slopes), component)
    return sub(outside, inside), inside


def outer_kernel(
    state,
    upright,
    turned,
    up_change,
    turned_change,
    codes,
    own_faces,
    high_crossing,
    high_faces,
    low_faces,
    early_faces,
    total,
    moved,
    fixed,
):
    block = lax.axis_index("blocks")
    first_of_row = (block > 0) & (block % ROW == 0)

    def ghost(group, axis, place, mirror, field):
        rows = 8 if axis != 1 else EDGE
        owner, source = codes[group, 0, 0:rows, :], codes[group, 1, 0:rows, :]
        number = face_planes(axis).index((field, mirror))

        def fetch(stored, index):
            there = face_rows(axis, stored)
            above = high_faces[there, :] + high_crossing[there, :]
            below = jnp.where(first_of_row, early_faces[there, :], low_faces[there, :])
            low, own, high = (
                jnp.take_along_axis(values, index, axis=0 if axis == 0 else 1)
                for values in (below, own_faces[there, :], above)
            )
            return jnp.where(owner == 0, low, jnp.where(owner == 1, own, high))

        if carried(axis, number):
            slot = source & 3 if axis == 0 else (source >> 4) & 3
            index = source | (3 if axis == 0 else 3 * EDGE)
            first, second, third = (fetch(number - 3 + carrier, index) for carrier in range(3))
            neighbour = jnp.where(slot == 0, first, jnp.where(slot == 1, second, third))
        else:
            neighbour = fetch(number, source)
        return jnp.where(owner == 3, face_plane(upright, turned, axis, field, place), neighbour)

    low_half = lanes_of(EDGE) < 64
    for field in range(FIELDS):
        fixed[field] = turned_change[field]

    cells = {
        number: [turned[field, band(number), :] for field in range(FIELDS)]
        for number in (0, 1, 2, 5, 6, 7)
    }
    ghosts = [[ghost(2, 1, depth, depth, field) for field in range(FIELDS)] for depth in range(2)]
    for side in range(2):
        numbers = (0, 1, 2) if side == 0 else (7, 6, 5)
        outside = []
        for depth in range(2):
            other = cells[7 - depth if side == 0 else depth]
            across = [pltpu.roll(value, 64, 1) for value in other]
            pair = (ghosts[depth], across) if side == 0 else (across, ghosts[depth])
            outside.append([jnp.where(low_half, a, b) for a, b in zip(*pair)])
        parts = outer_side(*outside, *(cells[number] for number in numbers), side, 2)
        for number, part in zip(numbers, parts):
            for field in range(FIELDS):
                fixed[field, band(number), :] += part[field]

    def comb_sides(square, axis, group, change):
        for side in range(2):
            numbers = (0, 1, 2) if side == 0 else (EDGE - 1, EDGE - 2, EDGE - 3)
            planes = [
                [square[field, comb(number), :] for field in range(FIELDS)] for number in numbers
            ]
            outside = [
                [
                    ghost(group + side, axis, 2 * side + depth, 2 * (1 - side) + depth, field)
                    for field in range(FIELDS)
                ]
                for depth in range(2)
            ]
            parts = outer_side(*outside, *planes, side, axis + 1)
            for number, part in zip(numbers, parts):
                for field in range(FIELDS):
                    change[field, comb(number), :] += part[field]

    comb_sides(turned, 2, 3, fixed)
    for field in range(FIELDS):
        total[field] = up_change[field] + fixed[field].T
    comb_sides(upright, 0, 0, total)

    for slot, field, half, here, there in square_moves():
        if slot == SLOTS - 1:
            moved[pl.ds(field * 2 * EDGE + half, EDGE, stride=2), :] = (
                state[here, :] - courant * total[field, there, :]
            )


def outer(*operands):
    vmem = pl.BlockSpec(memory_space=pltpu.VMEM)
    return pl.pallas_call(
        outer_kernel,
        out_shape=(SQUARES, jax.ShapeDtypeStruct((BLOCK_ROWS, LANES), jnp.float32)),
        in_specs=[vmem] * len(operands),
        out_specs=(vmem, vmem),
        scratch_shapes=[pltpu.VMEM(SQUARES.shape, jnp.float32)],
        compiler_params=pltpu.CompilerParams(vmem_limit_bytes=VMEM_LIMIT),
        name="outer",
    )(*operands)


def finish_kernel(rounds, state, total, counts, out, arrival):
    _, last_count, arrival_round = final_counts(counts, lax.axis_index("sub"), rounds)
    arrival[...] = jnp.full(arrival.shape, arrival_round, jnp.int32)
    for slot, field, _, here, there in square_moves():
        fresh = state[here, :] - courant * total[field, there, :]
        out[here, :] = jnp.where(slot < last_count, fresh, 0.0)


def finish(state, total, counts, rounds):
    vmem = pl.BlockSpec(memory_space=pltpu.VMEM)
    smem = pl.BlockSpec(memory_space=pltpu.SMEM)
    return pl.pallas_call(
        functools.partial(finish_kernel, rounds),
        out_shape=(
            jax.ShapeDtypeStruct(state.shape, jnp.float32),
            jax.ShapeDtypeStruct((8, LANES), jnp.int32),
        ),
        in_specs=[vmem, vmem, smem],
        out_specs=(vmem,) * 2,
        compiler_params=pltpu.CompilerParams(vmem_limit_bytes=VMEM_LIMIT),
        cost_estimate=pl.CostEstimate(flops=200_000, bytes_accessed=1_000_000, transcendentals=0),
        name="finish",
    )(state, total, counts)


def place_kernel(rounds, *refs):
    arrived, (arrival, _, out, sem) = refs[:rounds], refs[rounds:]
    arrived = dict(zip(SEND_ORDER, arrived))
    arrival_round = arrival[0, 0]
    for bit in range(rounds):
        @pl.when(arrival_round == bit)
        def _():
            copy = pltpu.make_async_copy(
                arrived[bit], out.at[pl.ds(BLOCK_ROWS, BLOCK_ROWS)], sem
            )
            copy.start()
            copy.wait()


def place(arrived, out, arrival):
    rounds = len(arrived)
    vmem = pl.BlockSpec(memory_space=pltpu.VMEM)
    anywhere = pl.BlockSpec(memory_space=pl.ANY)
    return pl.pallas_call(
        functools.partial(place_kernel, rounds),
        out_shape=jax.ShapeDtypeStruct(out.shape, out.dtype),
        in_specs=[vmem] * (rounds + 1) + [anywhere],
        out_specs=anywhere,
        scratch_shapes=[pltpu.SemaphoreType.DMA],
        input_output_aliases={rounds + 1: 0},
        compiler_params=pltpu.CompilerParams(vmem_limit_bytes=1024 * 1024),
        name="place",
    )(*arrived.values(), arrival, out)


def body(state, neighbours, counts):
    size = lax.axis_size("blocks")
    rounds = lax.axis_size("sub").bit_length() - 1
    shape = state.shape
    state = state.reshape(SLOTS * BLOCK_ROWS, LANES)
    links = jnp.transpose(neighbours.reshape(SLOTS, 6, 2), (0, 2, 1))
    upright, turned, faces = prepare(state)
    firsts = range(ROW, size, ROW)
    forward = [(i, i + 1) for i in range(size - 1) if i + 1 not in firsts]
    backward = [(i + 1, i) for i in range(size - 1) if i + 1 not in firsts]
    low = lax.ppermute(faces, "blocks", forward)
    high = lax.ppermute(faces, "blocks", backward)
    changes = interior(upright, turned, links)
    early = [(i, i - ROW + RELAY) for i in firsts] + [(i - 1, i) for i in firsts]
    relayed = lax.ppermute(faces, "blocks", early)
    held, *changes = lax.optimization_barrier((relayed, *changes))
    crossing = lax.ppermute(held, "blocks", [(i - ROW + RELAY, i - 1) for i in firsts])
    total, moved = outer(state, upright, turned, *changes, faces, crossing, high, low, relayed)
    arrived = {
        bit: lax.ppermute(
            moved, "sub", [(s, s ^ (1 << bit)) for s in range(lax.axis_size("sub"))]
        )
        for bit in SEND_ORDER
    }
    out, arrival = finish(state, total, counts, rounds)
    return place(arrived, out, arrival).reshape(shape)


def solution(mesh):
    return jax.shard_map(
        body,
        mesh=mesh,
        in_specs=(
            P("blocks", "sub", None, None, None),
            P("blocks", "sub", None, None, None),
            P("blocks", None),
        ),
        out_specs=P("blocks", "sub", None, None, None),
        check_vma=False,
    )
```

```python
import functools

import jax
import jax.numpy as jnp
from jax import lax
from jax.experimental import pallas as pl
from jax.experimental.pallas import tpu as pltpu
from jax.sharding import PartitionSpec as P

EDGE = 16
FIELDS = 5
SLOTS = 3
LANES = 128
BLOCK_ROWS = 2 * EDGE * FIELDS
OUTER = (0, 1, EDGE - 1, EDGE - 2)

SEND_ORDER = (0, 2, 1)
ROW = 16
RELAY = 7

heat_ratio = 1.4
courant = 0.07

VMEM_LIMIT = 16 * 1024 * 1024


def square_moves():
    for slot in range(SLOTS):
        for field in range(FIELDS):
            for half in range(2):
                here = pl.ds((slot * FIELDS + field) * 2 * EDGE + half, EDGE, stride=2)
                there = slice(half * 64 + slot * EDGE, half * 64 + (slot + 1) * EDGE)
                yield slot, field, half, here, there


def comb(number):
    return pl.ds(number, 8, stride=EDGE)


def band(number):
    return slice(number * EDGE, (number + 1) * EDGE)


def face_planes(axis):
    return [(field, place) for field in range(FIELDS) for place in range(2 if axis == 1 else 4)]


def carried(axis, number):
    return number % 4 == 3


def face_rows(axis, number):
    size = EDGE if axis == 1 else 8
    base = (0, 15 * 8, 15 * 8 + 8 * EDGE)[axis] + (number - number // 4) * size
    return slice(base, base + size)


FACE_ROWS = 15 * 8 + 8 * EDGE + 15 * 8


def face_plane(upright, turned, axis, field, place):
    if axis == 0:
        return upright[field, comb(OUTER[place]), :]
    if axis == 2:
        return turned[field, comb(OUTER[place]), :]
    return jnp.where(lanes_of(EDGE) < 64, turned[field, band(place), :], turned[field, band(7 - place), :])


def fourth_slot(axis):
    if axis == 0:
        return (lax.broadcasted_iota(jnp.int32, (8, LANES), 0) & 3) == 3
    return ((lanes_of(EDGE if axis == 1 else 8) >> 4) & 3) == 3


def lanes_of(rows):
    return lax.broadcasted_iota(jnp.int32, (rows, LANES), 1)


def primitives(cells):
    inverse = 1.0 / cells[0]
    v1, v2, v3 = cells[1] * inverse, cells[2] * inverse, cells[3] * inverse
    square = v1 * v1 + v2 * v2 + v3 * v3
    pressure = (heat_ratio - 1.0) * (cells[4] - 0.5 * cells[0] * square)
    return cells[0], v1, v2, v3, pressure


def prepare_kernel(state, upright, turned, faces):
    for half in range(2):
        for slot in range(SLOTS):
            cells = [
                state[pl.ds((slot * FIELDS + field) * 2 * EDGE + half, EDGE, stride=2), :]
                for field in range(FIELDS)
            ]
            for field, value in enumerate(primitives(cells)):
                upright[field, band(4 * half + slot), :] = value
                if slot == SLOTS - 1:
                    upright[field, band(4 * half + slot + 1), :] = value
    for field in range(FIELDS):
        turned[field] = upright[field].T
    for axis in range(3):
        planes = face_planes(axis)
        fourth = fourth_slot(axis)
        for number, (field, place) in enumerate(planes):
            if carried(axis, number):
                continue
            value = face_plane(upright, turned, axis, field, place)
            rider = number | 3
            if rider < len(planes):
                other = face_plane(upright, turned, axis, *planes[rider])
                shift = 3 - number % 4
                other = pltpu.roll(other, shift, 0) if axis == 0 else pltpu.roll(other, shift * EDGE, 1)
                value = jnp.where(fourth, other, value)
            faces[face_rows(axis, number), :] = value


SQUARES = jax.ShapeDtypeStruct((FIELDS, LANES, LANES), jnp.float32)


def prepare(state):
    return pl.pallas_call(
        prepare_kernel,
        out_shape=(SQUARES, SQUARES, jax.ShapeDtypeStruct((FACE_ROWS, LANES), jnp.float32)),
        compiler_params=pltpu.CompilerParams(vmem_limit_bytes=VMEM_LIMIT),
        name="prepare",
    )(state)


def minmod(first, second):
    return jnp.maximum(jnp.minimum(first, second), 0.0) + jnp.minimum(
        jnp.maximum(first, second), 0.0
    )


def side_speeds(prim, component):
    scaled = heat_ratio * prim[4]
    sound = scaled * lax.rsqrt(scaled * prim[0])
    return prim[component] - sound, prim[component] + sound


def hll_flux(left, right, component):
    slow_left, fast_left = side_speeds(left, component)
    slow_right, fast_right = side_speeds(right, component)
    slow = jnp.minimum(jnp.minimum(slow_left, slow_right), 0.0)
    fast = jnp.maximum(jnp.maximum(fast_left, fast_right), 0.0)
    inverse = 1.0 / (fast - slow)
    weight_left = fast * inverse
    weight_right = -slow * inverse
    product = slow * weight_left
    normal_left, normal_right = left[component], right[component]
    carry_left = weight_left * normal_left - product
    carry_right = weight_right * normal_right + product
    mass_left, mass_right = carry_left * left[0], carry_right * right[0]
    push_left, push_right = weight_left * left[4], weight_right * right[4]
    outputs = [mass_left + mass_right]
    for number in (1, 2, 3):
        value = mass_left * left[number] + mass_right * right[number]
        if number == component:
            value = value + (push_left + push_right)
        outputs.append(value)
    square_left = left[1] * left[1] + left[2] * left[2] + left[3] * left[3]
    square_right = right[1] * right[1] + right[2] * right[2] + right[3] * right[3]
    inner = 1.0 / (heat_ratio - 1.0)
    energy = 0.5 * (mass_left * square_left + mass_right * square_right)
    energy = energy + inner * (carry_left * left[4] + carry_right * right[4])
    energy = energy + (push_left * normal_left + push_right * normal_right)
    outputs.append(energy)
    return outputs


def half_slopes(before, here, after):
    return [0.5 * minmod(b - a, c - b) for a, b, c in zip(before, here, after)]


def add(first, second):
    return [a + b for a, b in zip(first, second)]


def sub(first, second):
    return [a - b for a, b in zip(first, second)]


GROUPS = 5


def ghost_codes(links, codes):
    lane = lanes_of(EDGE)
    row = lax.broadcasted_iota(jnp.int32, (EDGE, LANES), 0)

    def by_slot(slot, face, part):
        last = links[2, part, face]
        return jnp.where(slot == 0, links[0, part, face], jnp.where(slot == 1, links[1, part, face], last))

    for side in range(2):
        slot = row & 3
        codes[side, 0] = by_slot(slot, side, 0)
        codes[side, 1] = (row & 4) + by_slot(slot, side, 1)
    slot = (lane >> 4) & 3
    inside = lane & (EDGE - 1)
    low_half = lane < 64
    for part in range(2):
        value = jnp.where(low_half, by_slot(slot, 2, part), by_slot(slot, 3, part))
        if part == 1:
            value = 64 - (lane & 64) + value * EDGE + inside
        codes[2, part] = value
    for side in range(2):
        codes[3 + side, 0] = by_slot(slot, 4 + side, 0)
        codes[3 + side, 1] = (lane & 64) + by_slot(slot, 4 + side, 1) * EDGE + inside


def inner_line(cell, size, component, store):
    before, here = cell(0), cell(1)
    left, flux = None, None
    for number in range(1, size - 1):
        after = cell(number + 1)
        slopes = half_slopes(before, here, after)
        if left is not None:
            next_flux = hll_flux(left, sub(here, slopes), component)
            store(number - 1, next_flux if flux is None else sub(next_flux, flux))
            flux = next_flux
        left = add(here, slopes)
        before, here = here, after
    store(size - 2, [-value for value in flux])


def inner_kernel(upright, turned, links, up_change, turned_change, codes):
    def store_comb(change):
        def store(number, values):
            for field in range(FIELDS):
                change[field, comb(number), :] = values[field]

        return store

    def add_band(number, values):
        for field in range(FIELDS):
            turned_change[field, band(number), :] += values[field]

    nothing = [jnp.zeros((8, LANES), jnp.float32)] * FIELDS
    for change in (up_change, turned_change):
        for number in (0, EDGE - 1):
            store_comb(change)(number, nothing)
    inner_line(
        lambda number: [upright[field, comb(number), :] for field in range(FIELDS)],
        EDGE,
        1,
        store_comb(up_change),
    )
    inner_line(
        lambda number: [turned[field, comb(number), :] for field in range(FIELDS)],
        EDGE,
        3,
        store_comb(turned_change),
    )
    inner_line(
        lambda number: [turned[field, band(number), :] for field in range(FIELDS)],
        8,
        2,
        add_band,
    )
    ghost_codes(links, codes)


def interior(upright, turned, links):
    vmem = pl.BlockSpec(memory_space=pltpu.VMEM)
    return pl.pallas_call(
        inner_kernel,
        out_shape=(
            SQUARES,
            SQUARES,
            jax.ShapeDtypeStruct((GROUPS, 2, EDGE, LANES), jnp.int32),
        ),
        in_specs=[vmem, vmem, pl.BlockSpec(memory_space=pltpu.SMEM)],
        out_specs=(vmem,) * 3,
        compiler_params=pltpu.CompilerParams(vmem_limit_bytes=VMEM_LIMIT),
        cost_estimate=pl.CostEstimate(flops=6_000_000, bytes_accessed=3_000_000, transcendentals=0),
        name="interior",
    )(upright, turned, links)


def final_counts(counts, sub_index, rounds):
    size = counts.shape[-1]
    now = [counts[0, position] for position in range(size)]

    def own(values):
        picked = values[0]
        for position in range(1, size):
            picked = jnp.where(sub_index == position, values[position], picked)
        return picked

    start = own(now)
    arrival = jnp.int32(-1)
    for bit in range(rounds):
        gains = [
            jnp.maximum(now[p ^ (1 << bit)] - now[p], 0) // 2
            - jnp.maximum(now[p] - now[p ^ (1 << bit)], 0) // 2
            for p in range(size)
        ]
        arrival = jnp.where(own(gains) > 0, bit, arrival)
        now = [value + gain for value, gain in zip(now, gains)]
    return start, own(now), arrival


def outer_side(near, far, first, second, third, side, component):
    slopes = half_slopes(near, first, second)
    if side == 0:
        beyond = add(near, half_slopes(far, near, first))
        within = sub(second, half_slopes(first, second, third))
        outside = hll_flux(beyond, sub(first, slopes), component)
        inside = hll_flux(add(first, slopes), within, component)
        return sub(inside, outside), [-value for value in inside]
    slopes = half_slopes(second, first, near)
    beyond = sub(near, half_slopes(first, near, far))
    within = add(second, half_slopes(third, second, first))
    outside = hll_flux(add(first, slopes), beyond, component)
    inside = hll_flux(within, sub(first, slopes), component)
    return sub(outside, inside), inside


def outer_kernel(
    state,
    upright,
    turned,
    up_change,
    turned_change,
    codes,
    own_faces,
    high_crossing,
    high_faces,
    low_faces,
    early_faces,
    total,
    moved,
    fixed,
):
    block = lax.axis_index("blocks")
    first_of_row = (block > 0) & (block % ROW == 0)

    def ghost(group, axis, place, mirror, field):
        rows = 8 if axis != 1 else EDGE
        owner, source = codes[group, 0, 0:rows, :], codes[group, 1, 0:rows, :]
        number = face_planes(axis).index((field, mirror))

        def fetch(stored, index):
            there = face_rows(axis, stored)
            above = high_faces[there, :] + high_crossing[there, :]
            below = jnp.where(first_of_row, early_faces[there, :], low_faces[there, :])
            low, own, high = (
                jnp.take_along_axis(values, index, axis=0 if axis == 0 else 1)
                for values in (below, own_faces[there, :], above)
            )
            return jnp.where(owner == 0, low, jnp.where(owner == 1, own, high))

        if carried(axis, number):
            slot = source & 3 if axis == 0 else (source >> 4) & 3
            index = source | (3 if axis == 0 else 3 * EDGE)
            first, second, third = (fetch(number - 3 + carrier, index) for carrier in range(3))
            neighbour = jnp.where(slot == 0, first, jnp.where(slot == 1, second, third))
        else:
            neighbour = fetch(number, source)
        return jnp.where(owner == 3, face_plane(upright, turned, axis, field, place), neighbour)

    low_half = lanes_of(EDGE) < 64
    for field in range(FIELDS):
        fixed[field] = turned_change[field]

    cells = {
        number: [turned[field, band(number), :] for field in range(FIELDS)]
        for number in (0, 1, 2, 5, 6, 7)
    }
    ghosts = [[ghost(2, 1, depth, depth, field) for field in range(FIELDS)] for depth in range(2)]
    for side in range(2):
        numbers = (0, 1, 2) if side == 0 else (7, 6, 5)
        outside = []
        for depth in range(2):
            other = cells[7 - depth if side == 0 else depth]
            across = [pltpu.roll(value, 64, 1) for value in other]
            pair = (ghosts[depth], across) if side == 0 else (across, ghosts[depth])
            outside.append([jnp.where(low_half, a, b) for a, b in zip(*pair)])
        parts = outer_side(*outside, *(cells[number] for number in numbers), side, 2)
        for number, part in zip(numbers, parts):
            for field in range(FIELDS):
                fixed[field, band(number), :] += part[field]

    def comb_sides(square, axis, group, change):
        for side in range(2):
            numbers = (0, 1, 2) if side == 0 else (EDGE - 1, EDGE - 2, EDGE - 3)
            planes = [
                [square[field, comb(number), :] for field in range(FIELDS)] for number in numbers
            ]
            outside = [
                [
                    ghost(group + side, axis, 2 * side + depth, 2 * (1 - side) + depth, field)
                    for field in range(FIELDS)
                ]
                for depth in range(2)
            ]
            parts = outer_side(*outside, *planes, side, axis + 1)
            for number, part in zip(numbers, parts):
                for field in range(FIELDS):
                    change[field, comb(number), :] += part[field]

    comb_sides(turned, 2, 3, fixed)
    for field in range(FIELDS):
        total[field] = up_change[field] + fixed[field].T
    comb_sides(upright, 0, 0, total)

    for slot, field, half, here, there in square_moves():
        if slot == SLOTS - 1:
            moved[pl.ds(field * 2 * EDGE + half, EDGE, stride=2), :] = (
                state[here, :] - courant * total[field, there, :]
            )


def outer(*operands):
    vmem = pl.BlockSpec(memory_space=pltpu.VMEM)
    return pl.pallas_call(
        outer_kernel,
        out_shape=(SQUARES, jax.ShapeDtypeStruct((BLOCK_ROWS, LANES), jnp.float32)),
        in_specs=[vmem] * len(operands),
        out_specs=(vmem, vmem),
        scratch_shapes=[pltpu.VMEM(SQUARES.shape, jnp.float32)],
        compiler_params=pltpu.CompilerParams(vmem_limit_bytes=VMEM_LIMIT),
        name="outer",
    )(*operands)


def finish_kernel(rounds, state, total, counts, out, arrival):
    _, last_count, arrival_round = final_counts(counts, lax.axis_index("sub"), rounds)
    arrival[...] = jnp.full(arrival.shape, arrival_round, jnp.int32)
    for slot, field, _, here, there in square_moves():
        fresh = state[here, :] - courant * total[field, there, :]
        out[here, :] = jnp.where(slot < last_count, fresh, 0.0)


def finish(state, total, counts, rounds):
    vmem = pl.BlockSpec(memory_space=pltpu.VMEM)
    smem = pl.BlockSpec(memory_space=pltpu.SMEM)
    return pl.pallas_call(
        functools.partial(finish_kernel, rounds),
        out_shape=(
            jax.ShapeDtypeStruct(state.shape, jnp.float32),
            jax.ShapeDtypeStruct((8, LANES), jnp.int32),
        ),
        in_specs=[vmem, vmem, smem],
        out_specs=(vmem,) * 2,
        compiler_params=pltpu.CompilerParams(vmem_limit_bytes=VMEM_LIMIT),
        cost_estimate=pl.CostEstimate(flops=200_000, bytes_accessed=1_000_000, transcendentals=0),
        name="finish",
    )(state, total, counts)


def place_kernel(bits, *refs):
    arrived, (arrival, _, out, sem) = refs[: len(bits)], refs[len(bits) :]
    arrival_round = arrival[0, 0]
    for bit, buffer in zip(bits, arrived):
        @pl.when(arrival_round == bit)
        def _():
            copy = pltpu.make_async_copy(buffer, out.at[pl.ds(BLOCK_ROWS, BLOCK_ROWS)], sem)
            copy.start()
            copy.wait()


def place(arrived, bits, out, arrival):
    vmem = pl.BlockSpec(memory_space=pltpu.VMEM)
    anywhere = pl.BlockSpec(memory_space=pl.ANY)
    return pl.pallas_call(
        functools.partial(place_kernel, bits),
        out_shape=jax.ShapeDtypeStruct(out.shape, out.dtype),
        in_specs=[vmem] * (len(bits) + 1) + [anywhere],
        out_specs=anywhere,
        scratch_shapes=[pltpu.SemaphoreType.DMA],
        input_output_aliases={len(bits) + 1: 0},
        compiler_params=pltpu.CompilerParams(vmem_limit_bytes=1024 * 1024),
        name="place",
    )(*(arrived[bit] for bit in bits), arrival, out)


def body(state, neighbours, counts):
    size = lax.axis_size("blocks")
    rounds = lax.axis_size("sub").bit_length() - 1
    shape = state.shape
    state = state.reshape(SLOTS * BLOCK_ROWS, LANES)
    links = jnp.transpose(neighbours.reshape(SLOTS, 6, 2), (0, 2, 1))
    upright, turned, faces = prepare(state)
    firsts = range(ROW, size, ROW)
    forward = [(i, i + 1) for i in range(size - 1) if i + 1 not in firsts]
    backward = [(i + 1, i) for i in range(size - 1) if i + 1 not in firsts]
    low = lax.ppermute(faces, "blocks", forward)
    high = lax.ppermute(faces, "blocks", backward)
    changes = interior(upright, turned, links)
    early = [(i, i - ROW + RELAY) for i in firsts] + [(i - 1, i) for i in firsts]
    relayed = lax.ppermute(faces, "blocks", early)
    held, *changes = lax.optimization_barrier((relayed, *changes))
    crossing = lax.ppermute(held, "blocks", [(i - ROW + RELAY, i - 1) for i in firsts])
    total, moved = outer(state, upright, turned, *changes, faces, crossing, high, low, relayed)
    arrived = {
        bit: lax.ppermute(
            moved, "sub", [(s, s ^ (1 << bit)) for s in range(lax.axis_size("sub"))]
        )
        for bit in SEND_ORDER
    }
    out, arrival = finish(state, total, counts, rounds)
    out = place(arrived, SEND_ORDER[1:], out, arrival)
    return place(arrived, SEND_ORDER[:1], out, arrival).reshape(shape)


def solution(mesh):
    return jax.shard_map(
        body,
        mesh=mesh,
        in_specs=(
            P("blocks", "sub", None, None, None),
            P("blocks", "sub", None, None, None),
            P("blocks", None),
        ),
        out_specs=P("blocks", "sub", None, None, None),
        check_vma=False,
    )
```

```python
import functools

import jax
import jax.numpy as jnp
from jax import lax
from jax.experimental import pallas as pl
from jax.experimental.pallas import tpu as pltpu
from jax.sharding import PartitionSpec as P

EDGE = 16
FIELDS = 5
SLOTS = 3
LANES = 128
BLOCK_ROWS = 2 * EDGE * FIELDS
OUTER = (0, 1, EDGE - 1, EDGE - 2)

SEND_ORDER = (0, 2, 1)
ROW = 16
RELAY = 7

heat_ratio = 1.4
courant = 0.07

VMEM_LIMIT = 16 * 1024 * 1024


def square_moves():
    for slot in range(SLOTS):
        for field in range(FIELDS):
            for half in range(2):
                here = pl.ds((slot * FIELDS + field) * 2 * EDGE + half, EDGE, stride=2)
                there = slice(half * 64 + slot * EDGE, half * 64 + (slot + 1) * EDGE)
                yield slot, field, half, here, there


def comb(number):
    return pl.ds(number, 8, stride=EDGE)


def band(number):
    return slice(number * EDGE, (number + 1) * EDGE)


def face_planes(axis):
    return [(field, place) for field in range(FIELDS) for place in range(2 if axis == 1 else 4)]


def carried(axis, number):
    return number % 4 == 3


def face_rows(axis, number):
    size = EDGE if axis == 1 else 8
    base = (0, 15 * 8, 15 * 8 + 8 * EDGE)[axis] + (number - number // 4) * size
    return slice(base, base + size)


FACE_ROWS = 15 * 8 + 8 * EDGE + 15 * 8


def face_plane(upright, turned, axis, field, place):
    if axis == 0:
        return upright[field, comb(OUTER[place]), :]
    if axis == 2:
        return turned[field, comb(OUTER[place]), :]
    return jnp.where(lanes_of(EDGE) < 64, turned[field, band(place), :], turned[field, band(7 - place), :])


def fourth_slot(axis):
    if axis == 0:
        return (lax.broadcasted_iota(jnp.int32, (8, LANES), 0) & 3) == 3
    return ((lanes_of(EDGE if axis == 1 else 8) >> 4) & 3) == 3


def lanes_of(rows):
    return lax.broadcasted_iota(jnp.int32, (rows, LANES), 1)


def primitives(cells):
    inverse = 1.0 / cells[0]
    v1, v2, v3 = cells[1] * inverse, cells[2] * inverse, cells[3] * inverse
    square = v1 * v1 + v2 * v2 + v3 * v3
    pressure = (heat_ratio - 1.0) * (cells[4] - 0.5 * cells[0] * square)
    return cells[0], v1, v2, v3, pressure


def prepare_kernel(state, upright, turned, faces):
    for half in range(2):
        for slot in range(SLOTS):
            cells = [
                state[pl.ds((slot * FIELDS + field) * 2 * EDGE + half, EDGE, stride=2), :]
                for field in range(FIELDS)
            ]
            for field, value in enumerate(primitives(cells)):
                upright[field, band(4 * half + slot), :] = value
                if slot == SLOTS - 1:
                    upright[field, band(4 * half + slot + 1), :] = value
    for field in range(FIELDS):
        turned[field] = upright[field].T
    for axis in range(3):
        planes = face_planes(axis)
        fourth = fourth_slot(axis)
        for number, (field, place) in enumerate(planes):
            if carried(axis, number):
                continue
            value = face_plane(upright, turned, axis, field, place)
            rider = number | 3
            if rider < len(planes):
                other = face_plane(upright, turned, axis, *planes[rider])
                shift = 3 - number % 4
                other = pltpu.roll(other, shift, 0) if axis == 0 else pltpu.roll(other, shift * EDGE, 1)
                value = jnp.where(fourth, other, value)
            faces[face_rows(axis, number), :] = value


SQUARES = jax.ShapeDtypeStruct((FIELDS, LANES, LANES), jnp.float32)


def prepare(state):
    return pl.pallas_call(
        prepare_kernel,
        out_shape=(SQUARES, SQUARES, jax.ShapeDtypeStruct((FACE_ROWS, LANES), jnp.float32)),
        compiler_params=pltpu.CompilerParams(vmem_limit_bytes=VMEM_LIMIT),
        name="prepare",
    )(state)


def minmod(first, second):
    return jnp.maximum(jnp.minimum(first, second), 0.0) + jnp.minimum(
        jnp.maximum(first, second), 0.0
    )


def side_speeds(prim, component):
    scaled = heat_ratio * prim[4]
    sound = scaled * lax.rsqrt(scaled * prim[0])
    return prim[component] - sound, prim[component] + sound


def hll_flux(left, right, component):
    slow_left, fast_left = side_speeds(left, component)
    slow_right, fast_right = side_speeds(right, component)
    slow = jnp.minimum(jnp.minimum(slow_left, slow_right), 0.0)
    fast = jnp.maximum(jnp.maximum(fast_left, fast_right), 0.0)
    inverse = 1.0 / (fast - slow)
    weight_left = fast * inverse
    weight_right = -slow * inverse
    product = slow * weight_left
    normal_left, normal_right = left[component], right[component]
    carry_left = weight_left * normal_left - product
    carry_right = weight_right * normal_right + product
    mass_left, mass_right = carry_left * left[0], carry_right * right[0]
    push_left, push_right = weight_left * left[4], weight_right * right[4]
    outputs = [mass_left + mass_right]
    for number in (1, 2, 3):
        value = mass_left * left[number] + mass_right * right[number]
        if number == component:
            value = value + (push_left + push_right)
        outputs.append(value)
    square_left = left[1] * left[1] + left[2] * left[2] + left[3] * left[3]
    square_right = right[1] * right[1] + right[2] * right[2] + right[3] * right[3]
    inner = 1.0 / (heat_ratio - 1.0)
    energy = 0.5 * (mass_left * square_left + mass_right * square_right)
    energy = energy + inner * (carry_left * left[4] + carry_right * right[4])
    energy = energy + (push_left * normal_left + push_right * normal_right)
    outputs.append(energy)
    return outputs


def half_slopes(before, here, after):
    return [0.5 * minmod(b - a, c - b) for a, b, c in zip(before, here, after)]


def add(first, second):
    return [a + b for a, b in zip(first, second)]


def sub(first, second):
    return [a - b for a, b in zip(first, second)]


GROUPS = 5


def ghost_codes(links, codes):
    lane = lanes_of(EDGE)
    row = lax.broadcasted_iota(jnp.int32, (EDGE, LANES), 0)

    def by_slot(slot, face, part):
        last = links[2, part, face]
        return jnp.where(slot == 0, links[0, part, face], jnp.where(slot == 1, links[1, part, face], last))

    for side in range(2):
        slot = row & 3
        codes[side, 0] = by_slot(slot, side, 0)
        codes[side, 1] = (row & 4) + by_slot(slot, side, 1)
    slot = (lane >> 4) & 3
    inside = lane & (EDGE - 1)
    low_half = lane < 64
    for part in range(2):
        value = jnp.where(low_half, by_slot(slot, 2, part), by_slot(slot, 3, part))
        if part == 1:
            value = 64 - (lane & 64) + value * EDGE + inside
        codes[2, part] = value
    for side in range(2):
        codes[3 + side, 0] = by_slot(slot, 4 + side, 0)
        codes[3 + side, 1] = (lane & 64) + by_slot(slot, 4 + side, 1) * EDGE + inside


def inner_line(cell, size, component, store):
    before, here = cell(0), cell(1)
    left, flux = None, None
    for number in range(1, size - 1):
        after = cell(number + 1)
        slopes = half_slopes(before, here, after)
        if left is not None:
            next_flux = hll_flux(left, sub(here, slopes), component)
            store(number - 1, next_flux if flux is None else sub(next_flux, flux))
            flux = next_flux
        left = add(here, slopes)
        before, here = here, after
    store(size - 2, [-value for value in flux])


def inner_kernel(upright, turned, links, up_change, codes, turned_change):
    def store_comb(change):
        def store(number, values):
            for field in range(FIELDS):
                change[field, comb(number), :] = values[field]

        return store

    def add_band(number, values):
        for field in range(FIELDS):
            turned_change[field, band(number), :] += values[field]

    nothing = [jnp.zeros((8, LANES), jnp.float32)] * FIELDS
    for change in (up_change, turned_change):
        for number in (0, EDGE - 1):
            store_comb(change)(number, nothing)
    inner_line(
        lambda number: [upright[field, comb(number), :] for field in range(FIELDS)],
        EDGE,
        1,
        store_comb(up_change),
    )
    inner_line(
        lambda number: [turned[field, comb(number), :] for field in range(FIELDS)],
        EDGE,
        3,
        store_comb(turned_change),
    )
    inner_line(
        lambda number: [turned[field, band(number), :] for field in range(FIELDS)],
        8,
        2,
        add_band,
    )
    for field in range(FIELDS):
        up_change[field] += turned_change[field].T
    ghost_codes(links, codes)


def interior(upright, turned, links):
    vmem = pl.BlockSpec(memory_space=pltpu.VMEM)
    return pl.pallas_call(
        inner_kernel,
        out_shape=(SQUARES, jax.ShapeDtypeStruct((GROUPS, 2, EDGE, LANES), jnp.int32)),
        in_specs=[vmem, vmem, pl.BlockSpec(memory_space=pltpu.SMEM)],
        out_specs=(vmem,) * 2,
        scratch_shapes=[pltpu.VMEM(SQUARES.shape, jnp.float32)],
        compiler_params=pltpu.CompilerParams(vmem_limit_bytes=VMEM_LIMIT),
        cost_estimate=pl.CostEstimate(flops=6_000_000, bytes_accessed=3_000_000, transcendentals=0),
        name="interior",
    )(upright, turned, links)


def final_counts(counts, sub_index, rounds):
    size = counts.shape[-1]
    now = [counts[0, position] for position in range(size)]

    def own(values):
        picked = values[0]
        for position in range(1, size):
            picked = jnp.where(sub_index == position, values[position], picked)
        return picked

    start = own(now)
    arrival = jnp.int32(-1)
    for bit in range(rounds):
        gains = [
            jnp.maximum(now[p ^ (1 << bit)] - now[p], 0) // 2
            - jnp.maximum(now[p] - now[p ^ (1 << bit)], 0) // 2
            for p in range(size)
        ]
        arrival = jnp.where(own(gains) > 0, bit, arrival)
        now = [value + gain for value, gain in zip(now, gains)]
    return start, own(now), arrival


def outer_side(near, far, first, second, third, side, component):
    slopes = half_slopes(near, first, second)
    if side == 0:
        beyond = add(near, half_slopes(far, near, first))
        within = sub(second, half_slopes(first, second, third))
        outside = hll_flux(beyond, sub(first, slopes), component)
        inside = hll_flux(add(first, slopes), within, component)
        return sub(inside, outside), [-value for value in inside]
    slopes = half_slopes(second, first, near)
    beyond = sub(near, half_slopes(first, near, far))
    within = add(second, half_slopes(third, second, first))
    outside = hll_flux(add(first, slopes), beyond, component)
    inside = hll_flux(within, sub(first, slopes), component)
    return sub(outside, inside), inside


def outer_kernel(
    state,
    upright,
    turned,
    up_change,
    codes,
    own_faces,
    high_crossing,
    high_faces,
    low_faces,
    early_faces,
    total,
    moved,
    fixed,
):
    block = lax.axis_index("blocks")
    first_of_row = (block > 0) & (block % ROW == 0)

    def ghost(group, axis, place, mirror, field):
        rows = 8 if axis != 1 else EDGE
        owner, source = codes[group, 0, 0:rows, :], codes[group, 1, 0:rows, :]
        number = face_planes(axis).index((field, mirror))

        def fetch(stored, index):
            there = face_rows(axis, stored)
            above = high_faces[there, :] + high_crossing[there, :]
            below = jnp.where(first_of_row, early_faces[there, :], low_faces[there, :])
            low, own, high = (
                jnp.take_along_axis(values, index, axis=0 if axis == 0 else 1)
                for values in (below, own_faces[there, :], above)
            )
            return jnp.where(owner == 0, low, jnp.where(owner == 1, own, high))

        if carried(axis, number):
            slot = source & 3 if axis == 0 else (source >> 4) & 3
            index = source | (3 if axis == 0 else 3 * EDGE)
            first, second, third = (fetch(number - 3 + carrier, index) for carrier in range(3))
            neighbour = jnp.where(slot == 0, first, jnp.where(slot == 1, second, third))
        else:
            neighbour = fetch(number, source)
        return jnp.where(owner == 3, face_plane(upright, turned, axis, field, place), neighbour)

    low_half = lanes_of(EDGE) < 64
    for field in range(FIELDS):
        fixed[field] = jnp.zeros((LANES, LANES), jnp.float32)

    cells = {
        number: [turned[field, band(number), :] for field in range(FIELDS)]
        for number in (0, 1, 2, 5, 6, 7)
    }
    ghosts = [[ghost(2, 1, depth, depth, field) for field in range(FIELDS)] for depth in range(2)]
    for side in range(2):
        numbers = (0, 1, 2) if side == 0 else (7, 6, 5)
        outside = []
        for depth in range(2):
            other = cells[7 - depth if side == 0 else depth]
            across = [pltpu.roll(value, 64, 1) for value in other]
            pair = (ghosts[depth], across) if side == 0 else (across, ghosts[depth])
            outside.append([jnp.where(low_half, a, b) for a, b in zip(*pair)])
        parts = outer_side(*outside, *(cells[number] for number in numbers), side, 2)
        for number, part in zip(numbers, parts):
            for field in range(FIELDS):
                fixed[field, band(number), :] += part[field]

    def comb_sides(square, axis, group, change):
        for side in range(2):
            numbers = (0, 1, 2) if side == 0 else (EDGE - 1, EDGE - 2, EDGE - 3)
            planes = [
                [square[field, comb(number), :] for field in range(FIELDS)] for number in numbers
            ]
            outside = [
                [
                    ghost(group + side, axis, 2 * side + depth, 2 * (1 - side) + depth, field)
                    for field in range(FIELDS)
                ]
                for depth in range(2)
            ]
            parts = outer_side(*outside, *planes, side, axis + 1)
            for number, part in zip(numbers, parts):
                for field in range(FIELDS):
                    change[field, comb(number), :] += part[field]

    comb_sides(turned, 2, 3, fixed)
    for field in range(FIELDS):
        total[field] = up_change[field] + fixed[field].T
    comb_sides(upright, 0, 0, total)

    for slot, field, half, here, there in square_moves():
        if slot == SLOTS - 1:
            moved[pl.ds(field * 2 * EDGE + half, EDGE, stride=2), :] = (
                state[here, :] - courant * total[field, there, :]
            )


def outer(*operands):
    vmem = pl.BlockSpec(memory_space=pltpu.VMEM)
    return pl.pallas_call(
        outer_kernel,
        out_shape=(SQUARES, jax.ShapeDtypeStruct((BLOCK_ROWS, LANES), jnp.float32)),
        in_specs=[vmem] * len(operands),
        out_specs=(vmem, vmem),
        scratch_shapes=[pltpu.VMEM(SQUARES.shape, jnp.float32)],
        compiler_params=pltpu.CompilerParams(vmem_limit_bytes=VMEM_LIMIT),
        name="outer",
    )(*operands)


def finish_kernel(rounds, state, total, counts, out, arrival):
    _, last_count, arrival_round = final_counts(counts, lax.axis_index("sub"), rounds)
    arrival[...] = jnp.full(arrival.shape, arrival_round, jnp.int32)
    for slot, field, _, here, there in square_moves():
        fresh = state[here, :] - courant * total[field, there, :]
        out[here, :] = jnp.where(slot < last_count, fresh, 0.0)


def finish(state, total, counts, rounds):
    vmem = pl.BlockSpec(memory_space=pltpu.VMEM)
    smem = pl.BlockSpec(memory_space=pltpu.SMEM)
    return pl.pallas_call(
        functools.partial(finish_kernel, rounds),
        out_shape=(
            jax.ShapeDtypeStruct(state.shape, jnp.float32),
            jax.ShapeDtypeStruct((8, LANES), jnp.int32),
        ),
        in_specs=[vmem, vmem, smem],
        out_specs=(vmem,) * 2,
        compiler_params=pltpu.CompilerParams(vmem_limit_bytes=VMEM_LIMIT),
        cost_estimate=pl.CostEstimate(flops=200_000, bytes_accessed=1_000_000, transcendentals=0),
        name="finish",
    )(state, total, counts)


def place_kernel(bits, *refs):
    arrived, (arrival, _, out, sem) = refs[: len(bits)], refs[len(bits) :]
    arrival_round = arrival[0, 0]
    for bit, buffer in zip(bits, arrived):
        @pl.when(arrival_round == bit)
        def _():
            copy = pltpu.make_async_copy(buffer, out.at[pl.ds(BLOCK_ROWS, BLOCK_ROWS)], sem)
            copy.start()
            copy.wait()


def place(arrived, bits, out, arrival):
    vmem = pl.BlockSpec(memory_space=pltpu.VMEM)
    anywhere = pl.BlockSpec(memory_space=pl.ANY)
    return pl.pallas_call(
        functools.partial(place_kernel, bits),
        out_shape=jax.ShapeDtypeStruct(out.shape, out.dtype),
        in_specs=[vmem] * (len(bits) + 1) + [anywhere],
        out_specs=anywhere,
        scratch_shapes=[pltpu.SemaphoreType.DMA],
        input_output_aliases={len(bits) + 1: 0},
        compiler_params=pltpu.CompilerParams(vmem_limit_bytes=1024 * 1024),
        name="place",
    )(*(arrived[bit] for bit in bits), arrival, out)


def body(state, neighbours, counts):
    size = lax.axis_size("blocks")
    rounds = lax.axis_size("sub").bit_length() - 1
    shape = state.shape
    state = state.reshape(SLOTS * BLOCK_ROWS, LANES)
    links = jnp.transpose(neighbours.reshape(SLOTS, 6, 2), (0, 2, 1))
    upright, turned, faces = prepare(state)
    firsts = range(ROW, size, ROW)
    forward = [(i, i + 1) for i in range(size - 1) if i + 1 not in firsts]
    backward = [(i + 1, i) for i in range(size - 1) if i + 1 not in firsts]
    low = lax.ppermute(faces, "blocks", forward)
    high = lax.ppermute(faces, "blocks", backward)
    changes = interior(upright, turned, links)
    early = [(i, i - ROW + RELAY) for i in firsts] + [(i - 1, i) for i in firsts]
    relayed = lax.ppermute(faces, "blocks", early)
    held, *changes = lax.optimization_barrier((relayed, *changes))
    crossing = lax.ppermute(held, "blocks", [(i - ROW + RELAY, i - 1) for i in firsts])
    total, moved = outer(state, upright, turned, *changes, faces, crossing, high, low, relayed)
    arrived = {
        bit: lax.ppermute(
            moved, "sub", [(s, s ^ (1 << bit)) for s in range(lax.axis_size("sub"))]
        )
        for bit in SEND_ORDER
    }
    out, arrival = finish(state, total, counts, rounds)
    out = place(arrived, SEND_ORDER[1:], out, arrival)
    return place(arrived, SEND_ORDER[:1], out, arrival).reshape(shape)


def solution(mesh):
    return jax.shard_map(
        body,
        mesh=mesh,
        in_specs=(
            P("blocks", "sub", None, None, None),
            P("blocks", "sub", None, None, None),
            P("blocks", None),
        ),
        out_specs=P("blocks", "sub", None, None, None),
        check_vma=False,
    )
```
